128 devices in a mesh: boxes: 32 (over x, y, core), grp: 4 (over z).
Axes of the slice: x: 4, y: 4, z: 4, core: 2. Of those that a mesh axis runs over, the one named last changes fastest.
Arguments:
- charges: bfloat16 [16, 4194304], P(None, ('boxes', 'grp')), may hold values from -6 to 6
- leaf_basis: bfloat16 [16384, 64, 256], P(('boxes', 'grp')), may hold values from -0.375 to 0.375
- transfer0: bfloat16 [16384, 4096], P(('boxes', 'grp')), may hold values from -0.375 to 0.375
- transfer1: bfloat16 [2048, 4096], P(('boxes', 'grp')), may hold values from -0.375 to 0.375
- transfer2: bfloat16 [256, 4096], P(('boxes', 'grp')), may hold values from -0.375 to 0.375
- coupling: bfloat16 [4, 316, 4096], replicated, may hold values from -0.0546875 to 0.0546875
- lists0: int32 [16384, 189], P(('boxes', 'grp')), may hold values from -1 to 16383, as said below
- lists1: int32 [2048, 189], P(('boxes', 'grp')), may hold values from -1 to 2047, as said below
- lists2: int32 [256, 189], P(('boxes', 'grp')), may hold values from -1 to 255, as said below
- lists3: int32 [32, 189], P('boxes'), may hold values from -1 to 31, as said below
- kinds0: int32 [16384, 189], P(('boxes', 'grp')), may hold values from 0 to 315
- kinds1: int32 [2048, 189], P(('boxes', 'grp')), may hold values from 0 to 315
- kinds2: int32 [256, 189], P(('boxes', 'grp')), may hold values from 0 to 315
- kinds3: int32 [32, 189], P('boxes'), may hold values from 0 to 315
Outputs:
- potential: bfloat16 [16, 4194304], P(None, ('boxes', 'grp'))
The draws below stay inside these ranges and needn't reach their ends.
Inputs may be any that keep to these rules, and one draw needn't show every extreme that they name: `lists0`: each row names distinct leaf boxes by global Morton id, live entries first and -1 after them, at least one live. Device d owns leaf ids d * 128 to (d + 1) * 128 - 1, and its rows name boxes only of devices d - 13 to d + 13 and of the device half the devices away in Morton order; the lists of one device's leaf boxes name at most 32 distinct boxes of any one other device, and in every draw some pair of devices reaches 32. `lists1`: as for lists0, one level up: device d owns ids d * 16 onward, its rows name boxes only of devices d - 13 to d + 13 and of the device half the devices away, and at most 8 distinct boxes of one other device are named by one device's rows, reached in every draw. `lists2`: as for lists0, two levels up: device d owns ids d * 2 onward, its rows name boxes only of devices d - 13 to d + 13 and of the device half the devices away, and at most 2 distinct boxes of one other device are named by one device's rows, reached in every draw. `lists3`: each row names distinct boxes other than its own, live entries first and -1 after them, at least one live.
All inputs are finite; a program needn't handle non-finite values.
Results may differ from the reference program's by a relative error of at most 0.012.
Values may be sent and summed in bfloat16 or wider, within the bound.
A program may use at most 192 MiB of HBM per device.

```python
import jax
import jax.numpy as jnp
from jax import lax

LEAF = 256
RANK = 64
NVEC = 16
PARTNERS = 189
KINDS = 316
REACH = 13
LB_DEV = 128
NB0 = 16384
NB1 = 2048
NB2 = 256
NC = 32
POINTS = 4194304


def level_lists(key, box_count, capacity):
    devices = NB0 // LB_DEV
    entries = devices * box_count

    def one_device(device_key, device):
        key_width, key_start, key_pool, key_offset, key_live = jax.random.split(device_key, 5)
        peers = jnp.arange(devices, dtype=jnp.int32)
        widths = jax.random.randint(key_width, (devices,), (capacity + 1) // 2, capacity + 1)
        forced = (device + devices // 2) % devices
        widths = jnp.where(peers == forced, capacity, widths)
        widths = jnp.where(peers == device, box_count, widths)
        starts = jax.random.randint(key_start, (devices,), 0, box_count - widths + 1)
        column = jnp.arange(box_count, dtype=jnp.int32)
        box_ids = peers[:, None] * box_count + starts[:, None] + column[None, :]
        nearby = jnp.abs(peers - device) <= REACH
        usable = (column[None, :] < widths[:, None]) & (peers[:, None] != forced) & nearby[:, None]
        flat_ids = box_ids.reshape(-1)
        flat_usable = usable.reshape(-1)
        usable_count = jnp.sum(flat_usable.astype(jnp.int32))
        noise_bits = jax.random.randint(key_pool, (entries,), 0, 1024)
        order_key = jnp.where(flat_usable, noise_bits, 1024) * entries + jnp.arange(entries, dtype=jnp.int32)
        pool_ids = flat_ids[jnp.argsort(order_key)]
        highest = jnp.minimum(PARTNERS, usable_count + 1)
        live = jax.random.randint(key_live, (box_count,), highest // 2, highest + 1)
        offset = jax.random.randint(key_offset, (box_count,), 0, usable_count)
        steps_run = jnp.arange(PARTNERS - 1, dtype=jnp.int32)
        run_ids = pool_ids[(offset[:, None] + steps_run[None, :]) % usable_count]
        forced_ids = forced * box_count + starts[forced] + column % capacity
        joined = jnp.concatenate([forced_ids[:, None], run_ids], axis=1)
        keep = jnp.arange(PARTNERS, dtype=jnp.int32)[None, :] < live[:, None]
        return jnp.where(keep, joined, -1).astype(jnp.int32)
    device_keys = jax.random.split(key, devices)
    result = jax.vmap(one_device)(device_keys, jnp.arange(devices, dtype=jnp.int32))
    return result.reshape(entries, PARTNERS)


def draw_lists0(key, part):
    key = jax.random.fold_in(key, 11)
    return level_lists(key, LB_DEV, LB_DEV // 4)


def draw_lists1(key, part):
    key = jax.random.fold_in(key, 12)
    return level_lists(key, LB_DEV // 8, LB_DEV // 16)


def draw_lists2(key, part):
    key = jax.random.fold_in(key, 13)
    return level_lists(key, LB_DEV // 64, LB_DEV // 64)


def draw_lists3(key, part):
    key = jax.random.fold_in(key, 14)
    key_order, key_live = jax.random.split(key, 2)
    noise_bits = jax.random.randint(key_order, (NC, NC), 0, 1024)
    diagonal_mask = jnp.arange(NC)[:, None] == jnp.arange(NC)[None, :]
    order_key = jnp.where(diagonal_mask, 1024, noise_bits) * NC + jnp.arange(NC, dtype=jnp.int32)[None, :]
    ranking = jnp.argsort(order_key, axis=1).astype(jnp.int32)
    columns = min(PARTNERS, NC - 1)
    chosen = ranking[:, :columns]
    if columns < PARTNERS:
        chosen = jnp.concatenate([chosen, jnp.full((NC, PARTNERS - columns), -1, jnp.int32)], axis=1)
    live = jax.random.randint(key_live, (NC,), (columns + 1) // 2, columns + 1)
    keep = jnp.arange(PARTNERS, dtype=jnp.int32)[None, :] < live[:, None]
    return jnp.where(keep, chosen, -1).astype(jnp.int32)


def place_ends(drawn, stream_key, smallest, top_value):
    longest = drawn.shape.index(max(drawn.shape))
    spots = []
    for shift in (0, 1):
        where = [jax.random.randint(jax.random.fold_in(stream_key, axis), (), 0, length) for axis, length in enumerate(drawn.shape)]
        where[longest] = (where[longest] + shift) % drawn.shape[longest]
        spots.append(tuple(where))
    return drawn.at[spots[0]].set(smallest).at[spots[1]].set(top_value)


def block_scale(stream_key, extent, cuts, least, high):
    loudness, own = 1.0, jax.random.fold_in(stream_key, 6)
    for axis_at, parts in cuts:
        heights = jnp.exp(jax.random.uniform(jax.random.fold_in(own, axis_at), (parts,), jnp.float32, least / len(cuts), high / len(cuts)))
        loudness = loudness * jnp.repeat(heights, extent[axis_at] // parts).reshape([-1 if axis == axis_at else 1 for axis in range(len(extent))])
    return loudness


def centred(rng, dims, spread, most, shards=(), kind=jnp.bfloat16):
    level = block_scale(rng, dims, shards, -0.22, 0.18) if shards else 1.0
    values = jax.random.normal(rng, dims, jnp.float32) * spread * level
    return jnp.minimum(jnp.maximum(values, -most), most).astype(kind)


def setup_inputs(seed: int = 0) -> dict:
    splits = jax.random.split(jax.random.key(seed), 15)
    return {
        "charges": centred(splits[0], (NVEC, POINTS), 1.0, 6.0, ((1, 128),)),
        "leaf_basis": centred(splits[1], (NB0, RANK, LEAF), LEAF ** -0.5, 0.375, ((0, 128),)),
        "transfer0": centred(splits[2], (NB0, RANK * RANK), (4 * RANK) ** -0.5, 0.375, ((0, 128),)),
        "transfer1": centred(splits[3], (NB1, RANK * RANK), (4 * RANK) ** -0.5, 0.375, ((0, 128),)),
        "transfer2": centred(splits[4], (NB2, RANK * RANK), (4 * RANK) ** -0.5, 0.375, ((0, 128),)),
        "coupling": centred(splits[5], (4, KINDS, RANK * RANK), (RANK * PARTNERS) ** -0.5, 0.0546875),
        "lists0": draw_lists0(jax.random.fold_in(splits[14], 71), 0),
        "lists1": draw_lists1(jax.random.fold_in(splits[14], 71), 0),
        "lists2": draw_lists2(jax.random.fold_in(splits[14], 71), 0),
        "lists3": draw_lists3(jax.random.fold_in(splits[14], 71), 0),
        "kinds0": place_ends(jax.random.randint(splits[10], (NB0, PARTNERS), 0, KINDS), jax.random.fold_in(splits[10], 1), 0, KINDS - 1).astype(jnp.int32),
        "kinds1": place_ends(jax.random.randint(splits[11], (NB1, PARTNERS), 0, KINDS), jax.random.fold_in(splits[11], 1), 0, KINDS - 1).astype(jnp.int32),
        "kinds2": place_ends(jax.random.randint(splits[12], (NB2, PARTNERS), 0, KINDS), jax.random.fold_in(splits[12], 1), 0, KINDS - 1).astype(jnp.int32),
        "kinds3": place_ends(jax.random.randint(splits[13], (NC, PARTNERS), 0, KINDS), jax.random.fold_in(splits[13], 1), 0, KINDS - 1).astype(jnp.int32),
    }


def lift(transfer, children):
    matrices = transfer.astype(jnp.float32).reshape(-1, RANK, RANK)
    terms = jnp.einsum('bpc,bcv->bpv', matrices, children.astype(jnp.float32))
    return jnp.sum(terms.reshape(-1, 8, RANK, NVEC), axis=1).astype(jnp.bfloat16)


def far_field(table, partner_ids, slot_kinds, couple):
    rows_table = table.shape[0]
    extended = jnp.concatenate([table.reshape(rows_table, RANK * NVEC), jnp.zeros((1, RANK * NVEC), table.dtype)], axis=0)
    places = jnp.where(partner_ids >= 0, partner_ids, rows_table).astype(jnp.int32)
    rows_total = partner_ids.shape[0]
    block_rows = min(64, rows_total)

    def one_block(pair):
        chosen, which = pair
        matrices = couple[which].astype(jnp.float32).reshape(block_rows, PARTNERS, RANK, RANK)
        sources = extended[chosen].astype(jnp.float32).reshape(block_rows, PARTNERS, RANK, NVEC)
        return jnp.einsum('bprs,bpsv->brv', matrices, sources)

    result = lax.map(one_block, (places.reshape(-1, block_rows, PARTNERS), slot_kinds.reshape(-1, block_rows, PARTNERS)))
    return result.reshape(rows_total, RANK, NVEC)


def lower(transfer, parent_field, local_part):
    matrices = transfer.astype(jnp.float32).reshape(-1, RANK, RANK)
    parents = jnp.repeat(parent_field.astype(jnp.float32), 8, axis=0)
    return (local_part + jnp.einsum('bpc,bpv->bcv', matrices, parents)).astype(jnp.bfloat16)


def reference(charges, leaf_basis, transfer0, transfer1, transfer2, coupling, lists0, lists1, lists2, lists3, kinds0, kinds1, kinds2, kinds3):
    samples = charges.astype(jnp.float32).reshape(NVEC, NB0, LEAF)
    basis = leaf_basis.astype(jnp.float32)
    leaf_multi = jnp.einsum('bri,vbi->brv', basis, samples).astype(jnp.bfloat16)
    mid_multi = lift(transfer0, leaf_multi)
    upper_multi = lift(transfer1, mid_multi)
    coarse_multi = lift(transfer2, upper_multi)
    leaf_local = far_field(leaf_multi, lists0, kinds0, coupling[0])
    mid_local = far_field(mid_multi, lists1, kinds1, coupling[1])
    upper_local = far_field(upper_multi, lists2, kinds2, coupling[2])
    coarse_local = far_field(coarse_multi, lists3, kinds3, coupling[3])
    coarse_field = coarse_local.astype(jnp.bfloat16)
    upper_field = lower(transfer2, coarse_field, upper_local)
    mid_field = lower(transfer1, upper_field, mid_local)
    leaf_field = lower(transfer0, mid_field, leaf_local)
    potential = jnp.einsum('bri,brv->vbi', basis, leaf_field.astype(jnp.float32))
    return potential.astype(jnp.bfloat16).reshape(NVEC, POINTS)
```

```python
import functools

import jax
import jax.numpy as jnp
from jax import lax
from jax.experimental import pallas as pl
from jax.experimental.pallas import tpu as pltpu
from jax.sharding import PartitionSpec as P

BF = jnp.bfloat16
F32 = jnp.float32
I32 = jnp.int32
MESH = pl.DeviceIdType.MESH

DEV = 128
REACH = 13
SLOTS = 28
LEAFS = 128
ROOM = 32
SLOT_PAD = 192
TARGETS = 148
ZERO_ROW = SLOTS * LEAFS
MID_ROW = ZERO_ROW + 8
UPPER_ROW = MID_ROW + SLOTS * 16
COARSE_ROW = UPPER_ROW + SLOTS * 2
TABLE_ROWS = COARSE_ROW + 32
KIND_PAD = 320
VMEM = pl.BlockSpec(memory_space=pltpu.VMEM)
SMEM = pl.BlockSpec(memory_space=pltpu.SMEM)
NT = (((1,), (1,)), ((), ()))


def plan_kernel(l0, l1, l2, l3, k0, k1, k2, k3, rows_out, kinds_out, req_out):
    me = lax.axis_index("boxes") * 4 + lax.axis_index("grp")
    rows_out[...] = jnp.full(rows_out.shape, ZERO_ROW, I32)
    kinds_out[...] = jnp.zeros(kinds_out.shape, I32)
    start = 0
    for level, (lists, kinds, count, offset) in enumerate(
        ((l0, k0, 128, 0), (l1, k1, 16, MID_ROW), (l2, k2, 2, UPPER_ROW))
    ):
        ids = lists[...]
        whole = DEV * count
        rel = lax.rem(ids - (me - REACH) * count + whole, whole)
        far = (REACH + DEV // 2) * count
        rel = jnp.where(rel >= far, rel - far + (SLOTS - 1) * count, rel)
        rows_out[start : start + count, 0:189] = jnp.where(ids >= 0, rel + offset, ZERO_ROW)
        kinds_out[start : start + count, 0:189] = kinds[...] + level * KIND_PAD
        start += count
    ids = l3[...]
    rows_out[start : start + 1, 0:189] = jnp.where(ids >= 0, ids + COARSE_ROW, ZERO_ROW)
    kinds_out[start : start + 1, 0:189] = k3[...] + 3 * KIND_PAD

    sub_lo = lax.broadcasted_iota(I32, (LEAFS, SLOT_PAD), 0)
    sub_hi = lax.broadcasted_iota(I32, (32, SLOT_PAD), 0)

    def mark(t, seen):
        row = rows_out[pl.ds(t, 1), :]
        lo = jnp.where(sub_lo == (row & 127), 1.0, 0.0).astype(BF)
        hi = jnp.where(sub_hi == (row >> 7), 1.0, 0.0).astype(BF)
        return seen + lax.dot_general(hi, lo, NT, preferred_element_type=F32)

    seen = lax.fori_loop(0, LEAFS, mark, jnp.zeros((32, LEAFS), F32), unroll=4)
    needed = seen > 0.5
    lane = lax.broadcasted_iota(I32, (32, LEAFS), 1)
    upto = (
        lax.broadcasted_iota(I32, (LEAFS, LEAFS), 0) <= lax.broadcasted_iota(I32, (LEAFS, LEAFS), 1)
    )
    rank = jnp.dot(
        jnp.where(needed, 1.0, 0.0).astype(BF),
        jnp.where(upto, 1.0, 0.0).astype(BF),
        preferred_element_type=F32,
    )
    rank = jnp.where(needed, rank, 0.0)
    lane_f = lane.astype(F32)
    asked = jnp.zeros((32, LEAFS), F32)
    for q in range(ROOM):
        pick = jnp.sum(jnp.where(rank == q + 1.0, lane_f, 0.0), axis=1, keepdims=True)
        asked = jnp.where(lane == q, pick, asked)
    asked = asked.astype(I32)
    for h in range(SLOTS):
        req_out[h] = jnp.broadcast_to(asked[h : h + 1, :], (8, LEAFS))


def plan(lists, kinds):
    return pl.pallas_call(
        plan_kernel,
        out_shape=(
            jax.ShapeDtypeStruct((TARGETS, SLOT_PAD), I32),
            jax.ShapeDtypeStruct((TARGETS, SLOT_PAD), I32),
            jax.ShapeDtypeStruct((SLOTS, 8, 128), I32),
        ),
        in_specs=[VMEM] * 8,
        out_specs=[VMEM] * 3,
        compiler_params=pltpu.CompilerParams(vmem_limit_bytes=32 << 20),
        name="plan",
    )(*lists, *kinds)


def slot_of(i):
    return i + (i + 15) // 28


def offset_of(p):
    return p - REACH + (DEV // 2 - SLOTS + 1 + REACH) * (p // (SLOTS - 1))


def exchange_kernel(
    req, leaf, mu, part,
    leaf_out, mu_out, coarse_out,
    asked_v, asked_s, send, zbuf,
    req_ss, req_rs, loc_s, leaf_ss, leaf_rs, mu_ss, mu_rs, z_ss, z_rs, y_ss, y_rs, x_ss, x_rs,
):
    box = lax.axis_index("boxes")
    grp = lax.axis_index("grp")
    me = box * 4 + grp
    bx = box // 8
    by = box % 8

    def there(p):
        t = (me + offset_of(p) + DEV) % DEV
        return (t // 4, t % 4)

    def back(p):
        t = (me - offset_of(p) + DEV) % DEV
        return (t // 4, t % 4)

    def z_peer(i):
        return (box, (grp + i) % 4)

    def y_peer(i):
        return (bx * 8 + (by + i) % 8, grp)

    def x_peer(i):
        return (((bx + i) % 4) * 8 + by, grp)

    barrier = pltpu.get_barrier_semaphore()

    def greet(to, first, count):
        def one(i, c):
            pl.semaphore_signal(barrier, inc=1, device_id=to(i + first), device_id_type=MESH)
            return c

        lax.fori_loop(0, count, one, 0)

    greet(lambda i: there(slot_of(i)), 0, SLOTS - 1)
    greet(z_peer, 1, 3)
    greet(y_peer, 1, 7)
    greet(x_peer, 1, 3)
    pl.semaphore_wait(barrier, SLOTS - 1 + 13)

    def copy(src, dst, ss, rs, to):
        return pltpu.make_async_remote_copy(
            src_ref=src, dst_ref=dst, send_sem=ss, recv_sem=rs, device_id=to, device_id_type=MESH
        )

    def req_copy(p):
        return copy(req.at[p], asked_v.at[p], req_ss.at[p], req_rs.at[p], there(p))

    def leaf_copy(p):
        return copy(send.at[p], leaf_out.at[p], leaf_ss.at[p], leaf_rs.at[p], back(p))

    def mu_copy(p):
        return copy(mu, mu_out.at[p], mu_ss.at[p], mu_rs.at[p], back(p))

    def z_copy(i):
        return copy(part, zbuf.at[grp], z_ss.at[i], z_rs.at[i], z_peer(i))

    def y_copy(i):
        own = coarse_out.at[box]
        return copy(own, own, y_ss.at[i], y_rs.at[i], y_peer(i))

    def x_copy(i):
        own = coarse_out.at[pl.ds(bx * 8, 8)]
        return copy(own, own, x_ss.at[i], x_rs.at[i], x_peer(i))

    def each(count, first, act):
        def one(i, c):
            act(i + first)
            return c

        lax.fori_loop(0, count, one, 0)

    each(SLOTS - 1, 0, lambda i: req_copy(slot_of(i)).start())
    each(3, 1, lambda i: z_copy(i).start())
    each(SLOTS - 1, 0, lambda i: mu_copy(slot_of(i)).start())

    left = lax.broadcasted_iota(I32, (16, 128), 1) < 64

    def serve(i):
        p = slot_of(i)
        req_copy(p).wait_recv()
        local = pltpu.make_async_copy(asked_v.at[p], asked_s.at[p], loc_s.at[p])
        local.start()
        local.wait()
        for q in range(ROOM // 2):
            a = leaf[asked_s[p, 0, 2 * q]]
            b = leaf[asked_s[p, 0, 2 * q + 1]]
            send[p, q * 16 : (q + 1) * 16, :] = jnp.where(left, a, b)
        leaf_copy(p).start()

    each(SLOTS - 1, 0, serve)

    zbuf[grp] = part[...]
    each(3, 1, lambda i: z_copy(i).wait())
    coarse_out[box] = (zbuf[0] + zbuf[1] + zbuf[2] + zbuf[3]).astype(BF)
    each(7, 1, lambda i: y_copy(i).start())
    each(7, 1, lambda i: y_copy(i).wait())
    each(3, 1, lambda i: x_copy(i).start())
    each(3, 1, lambda i: x_copy(i).wait())

    each(SLOTS - 1, 0, lambda i: req_copy(slot_of(i)).wait_send())
    each(SLOTS - 1, 0, lambda i: mu_copy(slot_of(i)).wait())
    each(SLOTS - 1, 0, lambda i: leaf_copy(slot_of(i)).wait())


def exchange(req, leaf_twice, mu, part):
    sem = pltpu.SemaphoreType.DMA
    return pl.pallas_call(
        exchange_kernel,
        out_shape=(
            jax.ShapeDtypeStruct((SLOTS, 256, 128), BF),
            jax.ShapeDtypeStruct((SLOTS, 144, 128), BF),
            jax.ShapeDtypeStruct((32, 16, 128), BF),
        ),
        in_specs=[VMEM] * 4,
        out_specs=[VMEM] * 3,
        scratch_shapes=[
            pltpu.VMEM((SLOTS, 8, 128), I32),
            pltpu.SMEM((SLOTS, 8, 128), I32),
            pltpu.VMEM((SLOTS, 256, 128), BF),
            pltpu.VMEM((4, 16, 128), F32),
        ]
        + [sem((SLOTS,))] * 7
        + [sem((8,))] * 6,
        compiler_params=pltpu.CompilerParams(
            collective_id=0, has_side_effects=True, vmem_limit_bytes=32 << 20
        ),
        name="exchange",
    )(req, leaf_twice, mu, part)


def turn_kernel(coupling, out, rows):
    left = lax.broadcasted_iota(I32, (16, 128), 1) < 64
    for k in range(5):

        def spread(c, _, k=k):
            tile = coupling[0, k * 16 : (k + 1) * 16, pl.ds(pl.multiple_of(c * 128, 128), 128)]
            tile = tile.astype(F32)
            rows[pl.ds(k * 1024 + 2 * c, 16, stride=64), :] = jnp.where(left, tile, 0.0)
            rows[pl.ds(k * 1024 + 2 * c + 1, 16, stride=64), :] = jnp.where(left, 0.0, tile)
            return 0

        lax.fori_loop(0, 32, spread, 0, unroll=8)
    lane = lax.broadcasted_iota(I32, (32, 128), 1)
    low = jnp.where((lane & 31) == lax.broadcasted_iota(I32, (32, 128), 0), 1.0, 0.0).astype(BF)
    lower_half = (lax.broadcasted_iota(I32, (64, 128), 1) & 32) == 0

    def turn(i, _):
        parts = []
        for j in range(2):
            a = rows[pl.ds(pl.multiple_of((2 * i + j) * 64, 64), 64), :]
            parts += [jnp.where(lower_half, a, 0.0), jnp.where(lower_half, 0.0, a)]
        right = jnp.concatenate(parts, axis=0).astype(BF)
        w = lax.dot_general(low, right, NT, preferred_element_type=F32).astype(BF)
        out[2 * i] = w[:, :128]
        out[2 * i + 1] = w[:, 128:]
        return 0

    lax.fori_loop(0, 40, turn, 0, unroll=8)


def turn(coupling):
    return pl.pallas_call(
        turn_kernel,
        out_shape=jax.ShapeDtypeStruct((4 * KIND_PAD, 32, 128), BF),
        grid=(4, 4),
        in_specs=[pl.BlockSpec((1, 80, 4096), lambda i, j: (i, j, 0))],
        out_specs=pl.BlockSpec((80, 32, 128), lambda i, j: (i * 4 + j, 0, 0)),
        scratch_shapes=[pltpu.VMEM((80 * 64, 128), F32)],
        compiler_params=pltpu.CompilerParams(vmem_limit_bytes=32 << 20),
        name="turn",
    )(coupling)


def far_kernel(
    rows_idx, kinds_idx, req, own_leaf, own_mu, leaf_in, mu_in, coarse_in, weights, out, table
):
    l = lax.broadcasted_iota(I32, (128, 512), 0)
    n = lax.broadcasted_iota(I32, (128, 512), 1)
    spread = jnp.where(l == (n >> 7) * 32 + (n & 31), 1.0, 0.0).astype(BF)
    table[ZERO_ROW] = jnp.zeros((32, 128), BF)

    def fill(block, places):
        y = jnp.dot(block, spread, preferred_element_type=F32).astype(BF)
        for i, (a, b) in enumerate(places):
            s = slice(i * 16, (i + 1) * 16)
            table[a] = jnp.concatenate([y[s, 0:128], y[s, 128:256]], axis=0)
            if b is not None:
                table[b] = jnp.concatenate([y[s, 256:384], y[s, 384:512]], axis=0)

    def mu_places(p):
        mid = [(MID_ROW + p * 16 + 2 * i, MID_ROW + p * 16 + 2 * i + 1) for i in range(8)]
        return mid + [(UPPER_ROW + p * 2, UPPER_ROW + p * 2 + 1)]

    def peer(i, c):
        p = slot_of(i)
        fill(
            leaf_in[p],
            [(p * LEAFS + req[p, 0, 2 * q], p * LEAFS + req[p, 0, 2 * q + 1]) for q in range(16)],
        )
        fill(mu_in[p], mu_places(p))
        return c

    lax.fori_loop(0, SLOTS - 1, peer, 0)
    fill(own_mu[...], mu_places(REACH))

    def own(i, c):
        base = REACH * LEAFS + i * 32
        fill(
            own_leaf[pl.ds(pl.multiple_of(i * 256, 256), 256), :],
            [(base + 2 * q, base + 2 * q + 1) for q in range(16)],
        )
        return c

    lax.fori_loop(0, 4, own, 0)

    def coarse(i, c):
        fill(
            coarse_in[pl.ds(pl.multiple_of(i * 128, 128), 128), :],
            [(COARSE_ROW + i * 8 + q, None) for q in range(8)],
        )
        return c

    lax.fori_loop(0, 4, coarse, 0)

    lane = lax.broadcasted_iota(I32, (32, 128), 1)
    m1, m2, m3 = lane < 32, lane < 64, lane < 96
    left = lax.broadcasted_iota(I32, (16, 128), 1) < 64

    def merge(a, b, c, d):
        return jnp.where(m2, jnp.where(m1, a, b), jnp.where(m3, c, d))

    def one(t):
        acc = None
        for b in range(SLOT_PAD // 16):
            cols, quads = [], []
            for g in range(2):
                base = b * 16 + g * 8
                cols.append(
                    jnp.concatenate([weights[kinds_idx[t, base + j]] for j in range(8)], axis=0)
                )
                quads.append(
                    jnp.concatenate(
                        [
                            merge(*[table[rows_idx[t, base + q * 4 + i]] for i in range(4)])
                            for q in range(2)
                        ],
                        axis=1,
                    )
                )
            d = jnp.dot(
                jnp.concatenate(quads, axis=0),
                jnp.concatenate(cols, axis=1),
                preferred_element_type=F32,
            )
            acc = d if acc is None else acc + d
        u = jnp.where(
            left, acc[0:16, 0:128] + acc[32:48, 128:256], acc[16:32, 0:128] + acc[48:64, 128:256]
        )
        out[t] = (u + pltpu.roll(u, 64, 1))[:, :64]

    def four(i, c):
        for k in range(4):
            one(i * 4 + k)
        return c

    lax.fori_loop(0, TARGETS // 4, four, 0)


def far(rows_idx, kinds_idx, req, own_leaf, own_mu, leaf_in, mu_in, coarse_in, weights):
    return pl.pallas_call(
        far_kernel,
        out_shape=jax.ShapeDtypeStruct((TARGETS, 16, 64), F32),
        in_specs=[SMEM] * 3 + [VMEM] * 6,
        out_specs=VMEM,
        scratch_shapes=[pltpu.VMEM((TABLE_ROWS, 32, 128), BF)],
        compiler_params=pltpu.CompilerParams(vmem_limit_bytes=60 << 20),
        name="far",
    )(rows_idx, kinds_idx, req, own_leaf, own_mu, leaf_in, mu_in, coarse_in, weights)


def pairs(blocks):
    n = blocks.shape[0]
    return blocks.reshape(n // 2, 2, 16, 64).transpose(0, 2, 1, 3).reshape(n * 8, 128)


def lift(matrices, children):
    terms = jnp.einsum("bpc,bvc->bvp", matrices, children, preferred_element_type=F32)
    return terms


def lower(matrices, parents, local):
    terms = jnp.einsum("bpc,bvp->bvc", matrices, parents, preferred_element_type=F32)
    return (local + terms).astype(BF)


def on_device(
    charges, leaf_basis, transfer0, transfer1, transfer2, coupling,
    lists0, lists1, lists2, lists3, kinds0, kinds1, kinds2, kinds3,
):
    member = lax.axis_index("grp")
    samples = charges.reshape(16, 128, 256)
    e0 = transfer0.reshape(128, 64, 64)
    e1 = transfer1.reshape(16, 64, 64)
    e2 = transfer2.reshape(2, 64, 64)
    leaf = jnp.einsum("bri,vbi->bvr", leaf_basis, samples, preferred_element_type=F32).astype(BF)
    mid = lift(e0, leaf).reshape(16, 8, 16, 64).sum(axis=1).astype(BF)
    upper = lift(e1, mid).reshape(2, 8, 16, 64).sum(axis=1).astype(BF)
    part = lift(e2, upper).sum(axis=0)
    part = jnp.concatenate([part, jnp.zeros((16, 64), F32)], axis=1)
    leaf_twice = jnp.concatenate([leaf, leaf], axis=2)
    own_leaf = pairs(leaf)
    own_mu = jnp.concatenate([pairs(mid), pairs(upper)], axis=0)

    rows_idx, kinds_idx, req = plan(
        (lists0, lists1, lists2, lists3), (kinds0, kinds1, kinds2, kinds3)
    )
    leaf_in, mu_in, coarse_in = exchange(req, leaf_twice, own_mu, part)
    weights = turn(coupling)
    local = far(
        rows_idx, kinds_idx, req, own_leaf, own_mu, leaf_in, mu_in,
        coarse_in.reshape(512, 128), weights,
    )
    leaf_local = local[0:128]
    mid_local = local[128:144]
    upper_local = local[144:146]
    coarse_field = local[146:147].astype(BF)
    upper_field = lower(e2, jnp.repeat(coarse_field, 2, axis=0), upper_local)
    mid_field = lower(e1, jnp.repeat(upper_field, 8, axis=0), mid_local)
    leaf_field = lower(e0, jnp.repeat(mid_field, 8, axis=0), leaf_local)
    potential = jnp.einsum("bri,bvr->vbi", leaf_basis, leaf_field, preferred_element_type=F32)
    return potential.astype(BF).reshape(16, 128 * 256)


def solution(mesh):
    both = ("boxes", "grp")
    in_specs = (
        P(None, both),
        P(both, None, None),
        P(both, None),
        P(both, None),
        P(both, None),
        P(),
        P(both, None),
        P(both, None),
        P(both, None),
        P("boxes", None),
        P(both, None),
        P(both, None),
        P(both, None),
        P("boxes", None),
    )
    return jax.shard_map(
        on_device, mesh=mesh, in_specs=in_specs, out_specs=P(None, both), check_vma=False
    )
```

```python
import functools

import jax
import jax.numpy as jnp
from jax import lax
from jax.experimental import pallas as pl
from jax.experimental.pallas import tpu as pltpu
from jax.sharding import PartitionSpec as P

BF = jnp.bfloat16
F32 = jnp.float32
I32 = jnp.int32
MESH = pl.DeviceIdType.MESH

DEV = 128
REACH = 13
SLOTS = 28
LEAFS = 128
ROOM = 32
SLOT_PAD = 192
TARGETS = 148
ZERO_ROW = SLOTS * LEAFS
MID_ROW = ZERO_ROW + 8
UPPER_ROW = MID_ROW + SLOTS * 16
COARSE_ROW = UPPER_ROW + SLOTS * 2
TABLE_ROWS = COARSE_ROW + 32
KINDS = 316
VMEM = pl.BlockSpec(memory_space=pltpu.VMEM)
SMEM = pl.BlockSpec(memory_space=pltpu.SMEM)
NT = (((1,), (1,)), ((), ()))


def iota(shape, dim):
    return lax.broadcasted_iota(I32, shape, dim)


def plan_kernel(l0, l1, l2, l3, k0, k1, k2, k3, rows_flat, kinds_flat, req_out, rows_out, kinds_out):
    me = lax.axis_index("boxes") * 4 + lax.axis_index("grp")
    rows_out[...] = jnp.full(rows_out.shape, ZERO_ROW, I32)
    kinds_out[...] = jnp.zeros(kinds_out.shape, I32)
    start = 0
    for level, (lists, kinds, count, offset) in enumerate(
        ((l0, k0, 128, 0), (l1, k1, 16, MID_ROW), (l2, k2, 2, UPPER_ROW))
    ):
        ids = lists[...]
        whole = DEV * count
        rel = lax.rem(ids - (me - REACH) * count + whole, whole)
        far = (REACH + DEV // 2) * count
        rel = jnp.where(rel >= far, rel - far + (SLOTS - 1) * count, rel)
        rows_out[start : start + count, 0:189] = jnp.where(ids >= 0, rel + offset, ZERO_ROW)
        kinds_out[start : start + count, 0:189] = kinds[...] * 4 + level
        start += count
    ids = l3[...]
    rows_out[start : start + 1, 0:189] = jnp.where(ids >= 0, ids + COARSE_ROW, ZERO_ROW)
    kinds_out[start : start + 1, 0:189] = k3[...] * 4 + 3
    for flat, tiled in ((rows_flat, rows_out), (kinds_flat, kinds_out)):
        flat[pl.ds(0, TARGETS, stride=2), :] = tiled[:, 0:128]
        flat[pl.ds(1, TARGETS, stride=2), 0 : SLOT_PAD - 128] = tiled[:, 128:SLOT_PAD]

    sub_lo = iota((LEAFS, SLOT_PAD), 0)
    sub_hi = iota((32, SLOT_PAD), 0)

    def mark(t, seen):
        row = rows_out[pl.ds(t, 1), :]
        lo = jnp.where(sub_lo == (row & 127), 1.0, 0.0).astype(BF)
        hi = jnp.where(sub_hi == (row >> 7), 1.0, 0.0).astype(BF)
        return seen + lax.dot_general(hi, lo, NT, preferred_element_type=F32)

    seen = lax.fori_loop(0, LEAFS, mark, jnp.zeros((32, LEAFS), F32), unroll=4)
    needed = seen > 0.5
    lane = iota((32, LEAFS), 1)
    upto = (
        iota((LEAFS, LEAFS), 0) <= iota((LEAFS, LEAFS), 1)
    )
    rank = jnp.dot(
        jnp.where(needed, 1.0, 0.0).astype(BF),
        jnp.where(upto, 1.0, 0.0).astype(BF),
        preferred_element_type=F32,
    )
    rank = jnp.where(needed, rank, 0.0)
    lane_f = lane.astype(F32)
    asked = jnp.zeros((32, LEAFS), F32)
    for q in range(ROOM):
        pick = jnp.sum(jnp.where(rank == q + 1.0, lane_f, 0.0), axis=1, keepdims=True)
        asked = jnp.where(lane == q, pick, asked)
    asked = asked.astype(I32)
    for h in range(SLOTS):
        req_out[h] = jnp.broadcast_to(asked[h : h + 1, :], (8, LEAFS))


def plan(lists, kinds):
    return pl.pallas_call(
        plan_kernel,
        out_shape=(
            jax.ShapeDtypeStruct((2 * TARGETS, 128), I32),
            jax.ShapeDtypeStruct((2 * TARGETS, 128), I32),
            jax.ShapeDtypeStruct((SLOTS, 8, 128), I32),
        ),
        in_specs=[VMEM] * 8,
        out_specs=[VMEM] * 3,
        scratch_shapes=[pltpu.VMEM((TARGETS, SLOT_PAD), I32)] * 2,
        compiler_params=pltpu.CompilerParams(vmem_limit_bytes=32 << 20),
        name="plan",
    )(*lists, *kinds)


def turn(coupling, weights, first, last):
    eye = jnp.where(iota((128, 128), 0) == iota((128, 128), 1), 1.0, 0.0).astype(BF)
    row, col = iota((256, 256), 0), iota((256, 256), 1)
    fits = (col & 63) == 2 * ((row & 127) >> 2) + (row >> 7)
    pick = [
        jnp.where(fits & (((col >> 6) ^ h) == (row & 3)), 1.0, 0.0).astype(BF) for h in range(2)
    ]
    left = iota((32, 128), 1) < 64

    def step(i, _):
        rows = [[], []]
        for j in range(2):
            pair = coupling[pl.ds(i * 4 + 2 * j, 2)].reshape(256, 128)
            t = lax.dot_general(eye, pair, NT, preferred_element_type=F32).astype(BF)
            for k in range(2):
                y = t[:, k * 128 : (k + 1) * 128]
                for h in range(2):
                    a = y[h * 32 : h * 32 + 32]
                    b = y[64 + h * 32 : 64 + h * 32 + 32]
                    rows[h].append(jnp.concatenate([a, b], axis=1))
        half = [
            jnp.dot(jnp.concatenate(rows[h], axis=0), pick[h], preferred_element_type=F32).astype(BF)
            for h in range(2)
        ]
        for k in range(4):
            for p in range(2):
                a = half[0][k * 32 : k * 32 + 32, p * 128 : (p + 1) * 128]
                b = half[1][k * 32 : k * 32 + 32, p * 128 : (p + 1) * 128]
                weights[i * 4 + k, 2 * p] = jnp.where(left, a, b)
                weights[i * 4 + k, 2 * p + 1] = jnp.where(left, b, a)
        return 0

    lax.fori_loop(first, last, step, 0)


def slot_of(i):
    return i + (i + 15) // 28


def offset_of(p):
    return p - REACH + (DEV // 2 - SLOTS + 1 + REACH) * (p // (SLOTS - 1))


def exchange_kernel(
    req, leaf, mu, part, coupling,
    leaf_out, mu_out, coarse_out, weights,
    asked_v, asked_s, send, zbuf,
    req_ss, req_rs, loc_s, leaf_ss, leaf_rs, mu_ss, mu_rs, z_ss, z_rs, y_ss, y_rs, x_ss, x_rs,
):
    box = lax.axis_index("boxes")
    grp = lax.axis_index("grp")
    me = box * 4 + grp
    bx = box // 8
    by = box % 8

    def there(p):
        t = (me + offset_of(p) + DEV) % DEV
        return (t // 4, t % 4)

    def back(p):
        t = (me - offset_of(p) + DEV) % DEV
        return (t // 4, t % 4)

    def z_peer(i):
        return (box, (grp + i) % 4)

    def y_peer(i):
        return (bx * 8 + (by + i) % 8, grp)

    def x_peer(i):
        return (((bx + i) % 4) * 8 + by, grp)

    barrier = pltpu.get_barrier_semaphore()

    def greet(to, first, count):
        def one(i, c):
            pl.semaphore_signal(barrier, inc=1, device_id=to(i + first), device_id_type=MESH)
            return c

        lax.fori_loop(0, count, one, 0)

    greet(lambda i: there(slot_of(i)), 0, SLOTS - 1)
    greet(z_peer, 1, 3)
    greet(y_peer, 1, 7)
    greet(x_peer, 1, 3)
    pl.semaphore_wait(barrier, SLOTS - 1 + 13)

    def copy(src, dst, ss, rs, to):
        return pltpu.make_async_remote_copy(
            src_ref=src, dst_ref=dst, send_sem=ss, recv_sem=rs, device_id=to, device_id_type=MESH
        )

    def req_copy(p):
        return copy(req.at[p], asked_v.at[p], req_ss.at[p], req_rs.at[p], there(p))

    def leaf_copy(p):
        return copy(send.at[p], leaf_out.at[p], leaf_ss.at[p], leaf_rs.at[p], back(p))

    def mu_copy(p):
        return copy(mu, mu_out.at[p], mu_ss.at[p], mu_rs.at[p], back(p))

    def z_copy(i):
        return copy(part, zbuf.at[grp], z_ss.at[i], z_rs.at[i], z_peer(i))

    def y_copy(i):
        own = coarse_out.at[box]
        return copy(own, own, y_ss.at[i], y_rs.at[i], y_peer(i))

    def x_copy(i):
        own = coarse_out.at[pl.ds(bx * 8, 8)]
        return copy(own, own, x_ss.at[i], x_rs.at[i], x_peer(i))

    def each(count, first, act):
        def one(i, c):
            act(i + first)
            return c

        lax.fori_loop(0, count, one, 0)

    each(SLOTS - 1, 0, lambda i: req_copy(slot_of(i)).start())
    each(3, 1, lambda i: z_copy(i).start())
    each(SLOTS - 1, 0, lambda i: mu_copy(slot_of(i)).start())

    left = iota((16, 128), 1) < 64

    def serve(i):
        p = slot_of(i)
        req_copy(p).wait_recv()
        local = pltpu.make_async_copy(asked_v.at[p], asked_s.at[p], loc_s.at[p])
        local.start()
        local.wait()
        for q in range(ROOM // 2):
            a = leaf[asked_s[p, 0, 2 * q]]
            b = leaf[asked_s[p, 0, 2 * q + 1]]
            send[p, q * 16 : (q + 1) * 16, :] = jnp.where(left, a, b)
        leaf_copy(p).start()

    each(SLOTS - 1, 0, serve)

    zbuf[grp] = part[...]
    each(3, 1, lambda i: z_copy(i).wait())
    coarse_out[box] = (zbuf[0] + zbuf[1] + zbuf[2] + zbuf[3]).astype(BF)
    each(7, 1, lambda i: y_copy(i).start())
    turn(coupling, weights, 0, 39)
    each(7, 1, lambda i: y_copy(i).wait())
    each(3, 1, lambda i: x_copy(i).start())
    turn(coupling, weights, 39, 79)
    each(3, 1, lambda i: x_copy(i).wait())

    each(SLOTS - 1, 0, lambda i: req_copy(slot_of(i)).wait_send())
    each(SLOTS - 1, 0, lambda i: mu_copy(slot_of(i)).wait())
    each(SLOTS - 1, 0, lambda i: leaf_copy(slot_of(i)).wait())


def exchange(req, leaf_twice, mu, part, coupling):
    sem = pltpu.SemaphoreType.DMA
    return pl.pallas_call(
        exchange_kernel,
        out_shape=(
            jax.ShapeDtypeStruct((SLOTS, 256, 128), BF),
            jax.ShapeDtypeStruct((SLOTS, 144, 128), BF),
            jax.ShapeDtypeStruct((32, 16, 128), BF),
            jax.ShapeDtypeStruct((KINDS, 4, 32, 128), BF),
        ),
        in_specs=[VMEM] * 5,
        out_specs=[VMEM] * 4,
        scratch_shapes=[
            pltpu.VMEM((SLOTS, 8, 128), I32),
            pltpu.SMEM((SLOTS, 8, 128), I32),
            pltpu.VMEM((SLOTS, 256, 128), BF),
            pltpu.VMEM((4, 16, 128), F32),
        ]
        + [sem((SLOTS,))] * 7
        + [sem((8,))] * 6,
        compiler_params=pltpu.CompilerParams(
            collective_id=0, has_side_effects=True, vmem_limit_bytes=50 << 20
        ),
        name="exchange",
    )(req, leaf_twice, mu, part, coupling)


def far_kernel(
    rows_idx, kinds_idx, req, own_leaf, own_mu, leaf_in, mu_in, coarse_in, weights, out, table
):
    l = iota((128, 512), 0)
    n = iota((128, 512), 1)
    spread = jnp.where(l == (n >> 7) * 32 + (n & 31), 1.0, 0.0).astype(BF)
    table[ZERO_ROW] = jnp.zeros((32, 128), BF)

    def fill(block, places):
        y = jnp.dot(block, spread, preferred_element_type=F32).astype(BF)
        for i, (a, b, h) in enumerate(places):
            s = slice(i * 16, (i + 1) * 16)
            first = [y[s, 0:128], y[s, 128:256]]
            table[a] = jnp.concatenate([first[h], first[1 - h]], axis=0)
            if b is not None:
                last = [y[s, 256:384], y[s, 384:512]]
                table[b] = jnp.concatenate([last[h], last[1 - h]], axis=0)

    def mu_places(p):
        mid = [(MID_ROW + p * 16 + 2 * i, MID_ROW + p * 16 + 2 * i + 1, 1) for i in range(8)]
        return mid + [(UPPER_ROW + p * 2, UPPER_ROW + p * 2 + 1, 0)]

    def peer(i, c):
        p = slot_of(i)
        fill(
            leaf_in[p],
            [
                (p * LEAFS + req[p, 0, 2 * q], p * LEAFS + req[p, 0, 2 * q + 1], 0)
                for q in range(16)
            ],
        )
        fill(mu_in[p], mu_places(p))
        return c

    lax.fori_loop(0, SLOTS - 1, peer, 0)
    fill(own_mu[...], mu_places(REACH))

    def own(i, c):
        base = REACH * LEAFS + i * 32
        fill(
            own_leaf[pl.ds(pl.multiple_of(i * 256, 256), 256), :],
            [(base + 2 * q, base + 2 * q + 1, 0) for q in range(16)],
        )
        return c

    lax.fori_loop(0, 4, own, 0)

    def coarse(i, c):
        fill(
            coarse_in[pl.ds(pl.multiple_of(i * 128, 128), 128), :],
            [(COARSE_ROW + i * 8 + q, None, 1) for q in range(8)],
        )
        return c

    lax.fori_loop(0, 4, coarse, 0)

    lane = iota((32, 128), 1)
    m1, m2, m3 = lane < 32, lane < 64, lane < 96
    left = iota((16, 128), 1) < 64

    def merge(a, b, c, d):
        return jnp.where(m2, jnp.where(m1, a, b), jnp.where(m3, c, d))

    def one(t):
        acc = None
        for b in range(SLOT_PAD // 16):
            cols, quads = [], []
            for g in range(2):
                base = b * 16 + g * 8
                cols.append(
                    jnp.concatenate([weights[kinds_idx[t * 256 + base + j]] for j in range(8)], axis=0)
                )
                quads.append(
                    jnp.concatenate(
                        [
                            merge(*[table[rows_idx[t * 256 + base + q * 4 + i]] for i in range(4)])
                            for q in range(2)
                        ],
                        axis=1,
                    )
                )
            d = jnp.dot(
                jnp.concatenate(quads, axis=0),
                jnp.concatenate(cols, axis=1),
                preferred_element_type=F32,
            )
            acc = d if acc is None else acc + d
        u = jnp.where(
            left, acc[0:16, 0:128] + acc[32:48, 128:256], acc[16:32, 0:128] + acc[48:64, 128:256]
        )
        out[t] = (u + pltpu.roll(u, 64, 1))[:, :64]

    def four(i, c):
        for k in range(4):
            one(i * 4 + k)
        return c

    lax.fori_loop(0, TARGETS // 4, four, 0)


def far(rows_idx, kinds_idx, req, own_leaf, own_mu, leaf_in, mu_in, coarse_in, weights):
    return pl.pallas_call(
        far_kernel,
        out_shape=jax.ShapeDtypeStruct((TARGETS, 16, 64), F32),
        in_specs=[SMEM] * 3 + [VMEM] * 6,
        out_specs=VMEM,
        scratch_shapes=[pltpu.VMEM((TABLE_ROWS, 32, 128), BF)],
        compiler_params=pltpu.CompilerParams(vmem_limit_bytes=60 << 20),
        name="far",
    )(rows_idx, kinds_idx, req, own_leaf, own_mu, leaf_in, mu_in, coarse_in, weights)


def pairs(blocks):
    n = blocks.shape[0]
    return blocks.reshape(n // 2, 2, 16, 64).transpose(0, 2, 1, 3).reshape(n * 8, 128)


def lift(matrices, children):
    terms = jnp.einsum("bpc,bvc->bvp", matrices, children, preferred_element_type=F32)
    return terms


def lower(matrices, parents, local):
    terms = jnp.einsum("bpc,bvp->bvc", matrices, parents, preferred_element_type=F32)
    return (local + terms).astype(BF)


def on_device(
    charges, leaf_basis, transfer0, transfer1, transfer2, coupling,
    lists0, lists1, lists2, lists3, kinds0, kinds1, kinds2, kinds3,
):
    member = lax.axis_index("grp")
    samples = charges.reshape(16, 128, 256)
    e0 = transfer0.reshape(128, 64, 64)
    e1 = transfer1.reshape(16, 64, 64)
    e2 = transfer2.reshape(2, 64, 64)
    leaf = jnp.einsum("bri,vbi->bvr", leaf_basis, samples, preferred_element_type=F32).astype(BF)
    mid = lift(e0, leaf).reshape(16, 8, 16, 64).sum(axis=1).astype(BF)
    upper = lift(e1, mid).reshape(2, 8, 16, 64).sum(axis=1).astype(BF)
    part = lift(e2, upper).sum(axis=0)
    part = jnp.concatenate([part, jnp.zeros((16, 64), F32)], axis=1)
    leaf_twice = jnp.concatenate([leaf, leaf], axis=2)
    own_leaf = pairs(leaf)
    own_mu = jnp.concatenate([pairs(mid), pairs(upper)], axis=0)

    rows_idx, kinds_idx, req = plan(
        (lists0, lists1, lists2, lists3), (kinds0, kinds1, kinds2, kinds3)
    )
    by_kind = coupling.reshape(4, KINDS, 32, 128).transpose(1, 2, 0, 3).reshape(KINDS, 128, 128)
    leaf_in, mu_in, coarse_in, weights = exchange(req, leaf_twice, own_mu, part, by_kind)
    local = far(
        rows_idx.reshape(-1), kinds_idx.reshape(-1), req, own_leaf, own_mu, leaf_in, mu_in,
        coarse_in.reshape(512, 128), weights.reshape(4 * KINDS, 32, 128),
    )
    leaf_local = local[0:128]
    mid_local = local[128:144]
    upper_local = local[144:146]
    coarse_field = local[146:147].astype(BF)
    upper_field = lower(e2, jnp.repeat(coarse_field, 2, axis=0), upper_local)
    mid_field = lower(e1, jnp.repeat(upper_field, 8, axis=0), mid_local)
    leaf_field = lower(e0, jnp.repeat(mid_field, 8, axis=0), leaf_local)
    potential = jnp.einsum("bri,bvr->vbi", leaf_basis, leaf_field, preferred_element_type=F32)
    return potential.astype(BF).reshape(16, 128 * 256)


def solution(mesh):
    both = ("boxes", "grp")
    in_specs = (
        P(None, both),
        P(both, None, None),
        P(both, None),
        P(both, None),
        P(both, None),
        P(),
        P(both, None),
        P(both, None),
        P(both, None),
        P("boxes", None),
        P(both, None),
        P(both, None),
        P(both, None),
        P("boxes", None),
    )
    return jax.shard_map(
        on_device, mesh=mesh, in_specs=in_specs, out_specs=P(None, both), check_vma=False
    )
```

```python
import functools

import jax
import jax.numpy as jnp
from jax import lax
from jax.experimental import pallas as pl
from jax.experimental.pallas import tpu as pltpu
from jax.sharding import PartitionSpec as P

BF = jnp.bfloat16
F32 = jnp.float32
I32 = jnp.int32
MESH = pl.DeviceIdType.MESH

DEV = 128
REACH = 13
SLOTS = 28
LEAFS = 128
ROOM = 32
SLOT_PAD = 192
TARGETS = 148
ZERO_ROW = SLOTS * LEAFS
MID_ROW = ZERO_ROW + 8
UPPER_ROW = MID_ROW + SLOTS * 16
COARSE_ROW = UPPER_ROW + SLOTS * 2
TABLE_ROWS = COARSE_ROW + 32
KINDS = 316
VMEM = pl.BlockSpec(memory_space=pltpu.VMEM)
SMEM = pl.BlockSpec(memory_space=pltpu.SMEM)
NT = (((1,), (1,)), ((), ()))


def iota(shape, dim):
    return lax.broadcasted_iota(I32, shape, dim)


def plan_kernel(l0, l1, l2, l3, k0, k1, k2, k3, rows_flat, kinds_flat, req_out, meta, rows_out, kinds_out):
    me = lax.axis_index("boxes") * 4 + lax.axis_index("grp")
    rows_out[...] = jnp.full(rows_out.shape, ZERO_ROW, I32)
    kinds_out[...] = jnp.zeros(kinds_out.shape, I32)
    start = 0
    for level, (lists, kinds, count, offset) in enumerate(
        ((l0, k0, 128, 0), (l1, k1, 16, MID_ROW), (l2, k2, 2, UPPER_ROW))
    ):
        ids = lists[...]
        whole = DEV * count
        rel = lax.rem(ids - (me - REACH) * count + whole, whole)
        far = (REACH + DEV // 2) * count
        rel = jnp.where(rel >= far, rel - far + (SLOTS - 1) * count, rel)
        rows_out[start : start + count, 0:189] = jnp.where(ids >= 0, rel + offset, ZERO_ROW)
        kinds_out[start : start + count, 0:189] = kinds[...] * 4 + level
        start += count
    ids = l3[...]
    rows_out[start : start + 1, 0:189] = jnp.where(ids >= 0, ids + COARSE_ROW, ZERO_ROW)
    kinds_out[start : start + 1, 0:189] = k3[...] * 4 + 3
    for flat, tiled in ((rows_flat, rows_out), (kinds_flat, kinds_out)):
        flat[pl.ds(0, TARGETS, stride=2), :] = tiled[:, 0:128]
        flat[pl.ds(1, TARGETS, stride=2), 0 : SLOT_PAD - 128] = tiled[:, 128:SLOT_PAD]

    live = jnp.where(rows_out[...] != ZERO_ROW, 1.0, 0.0).astype(BF)
    down = jnp.dot(live, jnp.ones((SLOT_PAD, 256), BF), preferred_element_type=F32)[:, :TARGETS]
    across = lax.dot_general(jnp.ones((8, SLOT_PAD), BF), live, NT, preferred_element_type=F32)
    down = (down.astype(I32) + 15) >> 4
    across = (across[0:1].astype(I32) + 15) >> 4
    t_down, t_across = iota((TARGETS, TARGETS), 0), iota((TARGETS, TARGETS), 1)
    before = (across > down) | ((across == down) & (t_across < t_down))
    place = jnp.sum(jnp.where(before, 1.0, 0.0), axis=1, keepdims=True)
    here = place == t_across.astype(F32)
    order = jnp.sum(jnp.where(here, t_down.astype(F32), 0.0), axis=0, keepdims=True).astype(I32)
    meta[...] = jnp.zeros(meta.shape, I32)
    meta[0:1, 0:TARGETS] = order
    sub = iota((16, TARGETS), 0)
    over = jnp.sum(jnp.where(across > sub, 1.0, 0.0), axis=1, keepdims=True).astype(I32)
    ends = jnp.where(iota((16, 256), 1) == iota((16, 256), 0), (over + 3) >> 2, 0)
    meta[1:2, :] = jnp.sum(ends, axis=0, keepdims=True)

    sub_lo = iota((LEAFS, SLOT_PAD), 0)
    sub_hi = iota((32, SLOT_PAD), 0)

    def mark(t, seen):
        row = rows_out[pl.ds(t, 1), :]
        lo = jnp.where(sub_lo == (row & 127), 1.0, 0.0).astype(BF)
        hi = jnp.where(sub_hi == (row >> 7), 1.0, 0.0).astype(BF)
        return seen + lax.dot_general(hi, lo, NT, preferred_element_type=F32)

    seen = lax.fori_loop(0, LEAFS, mark, jnp.zeros((32, LEAFS), F32), unroll=4)
    needed = seen > 0.5
    lane = iota((32, LEAFS), 1)
    upto = (
        iota((LEAFS, LEAFS), 0) <= iota((LEAFS, LEAFS), 1)
    )
    rank = jnp.dot(
        jnp.where(needed, 1.0, 0.0).astype(BF),
        jnp.where(upto, 1.0, 0.0).astype(BF),
        preferred_element_type=F32,
    )
    rank = jnp.where(needed, rank, 0.0)
    lane_f = lane.astype(F32)
    asked = jnp.zeros((32, LEAFS), F32)
    for q in range(ROOM):
        pick = jnp.sum(jnp.where(rank == q + 1.0, lane_f, 0.0), axis=1, keepdims=True)
        asked = jnp.where(lane == q, pick, asked)
    asked = asked.astype(I32)
    for h in range(SLOTS):
        req_out[h] = asked[h : h + 1, :]


def plan(lists, kinds):
    return pl.pallas_call(
        plan_kernel,
        out_shape=(
            jax.ShapeDtypeStruct((2 * TARGETS, 128), I32),
            jax.ShapeDtypeStruct((2 * TARGETS, 128), I32),
            jax.ShapeDtypeStruct((SLOTS, 1, 128), I32),
            jax.ShapeDtypeStruct((8, 256), I32),
        ),
        in_specs=[VMEM] * 8,
        out_specs=[VMEM] * 4,
        scratch_shapes=[pltpu.VMEM((TARGETS, SLOT_PAD), I32)] * 2,
        compiler_params=pltpu.CompilerParams(vmem_limit_bytes=32 << 20),
        name="plan",
    )(*lists, *kinds)


def turn(coupling, weights, first, last):
    eye = jnp.where(iota((128, 128), 0) == iota((128, 128), 1), 1.0, 0.0).astype(BF)
    row, col = iota((256, 256), 0), iota((256, 256), 1)
    fits = (col & 63) == 2 * ((row & 127) >> 2) + (row >> 7)
    pick = [
        jnp.where(fits & (((col >> 6) ^ h) == (row & 3)), 1.0, 0.0).astype(BF) for h in range(2)
    ]
    left = iota((32, 128), 1) < 64

    def step(i, _):
        rows = [[], []]
        for j in range(2):
            pair = coupling[pl.ds(i * 4 + 2 * j, 2)].reshape(256, 128)
            t = lax.dot_general(eye, pair, NT, preferred_element_type=F32).astype(BF)
            for k in range(2):
                y = t[:, k * 128 : (k + 1) * 128]
                for h in range(2):
                    a = y[h * 32 : h * 32 + 32]
                    b = y[64 + h * 32 : 64 + h * 32 + 32]
                    rows[h].append(jnp.concatenate([a, b], axis=1))
        half = [
            jnp.dot(jnp.concatenate(rows[h], axis=0), pick[h], preferred_element_type=F32).astype(BF)
            for h in range(2)
        ]
        for k in range(4):
            for p in range(2):
                a = half[0][k * 32 : k * 32 + 32, p * 128 : (p + 1) * 128]
                b = half[1][k * 32 : k * 32 + 32, p * 128 : (p + 1) * 128]
                weights[i * 4 + k, 2 * p] = jnp.where(left, a, b)
                weights[i * 4 + k, 2 * p + 1] = jnp.where(left, b, a)
        return 0

    lax.fori_loop(first, last, step, 0)


def slot_of(i):
    return i + (i + 15) // 28


def offset_of(p):
    return p - REACH + (DEV // 2 - SLOTS + 1 + REACH) * (p // (SLOTS - 1))


def exchange_kernel(
    req, leaf, mu, part, coupling,
    leaf_out, mu_out, coarse_out, weights,
    asked_v, asked_s, send, zbuf,
    req_ss, req_rs, loc_s, leaf_ss, leaf_rs, mu_ss, mu_rs, z_ss, z_rs, y_ss, y_rs, x_ss, x_rs,
):
    box = lax.axis_index("boxes")
    grp = lax.axis_index("grp")
    me = box * 4 + grp
    bx = box // 8
    by = box % 8

    def there(p):
        t = (me + offset_of(p) + DEV) % DEV
        return (t // 4, t % 4)

    def back(p):
        t = (me - offset_of(p) + DEV) % DEV
        return (t // 4, t % 4)

    def z_peer(i):
        return (box, (grp + i) % 4)

    def y_peer(i):
        return (bx * 8 + (by + i) % 8, grp)

    def x_peer(i):
        return (((bx + i) % 4) * 8 + by, grp)

    barrier = pltpu.get_barrier_semaphore()

    def greet(to, first, count):
        def one(i, c):
            pl.semaphore_signal(barrier, inc=1, device_id=to(i + first), device_id_type=MESH)
            return c

        lax.fori_loop(0, count, one, 0)

    greet(lambda i: there(slot_of(i)), 0, SLOTS - 1)
    greet(z_peer, 1, 3)
    greet(y_peer, 1, 7)
    greet(x_peer, 1, 3)
    pl.semaphore_wait(barrier, SLOTS - 1 + 13)

    def copy(src, dst, ss, rs, to):
        return pltpu.make_async_remote_copy(
            src_ref=src, dst_ref=dst, send_sem=ss, recv_sem=rs, device_id=to, device_id_type=MESH
        )

    def req_copy(p):
        return copy(req.at[p], asked_v.at[p], req_ss.at[p], req_rs.at[p], there(p))

    def leaf_copy(p):
        return copy(send.at[p], leaf_out.at[p], leaf_ss.at[p], leaf_rs.at[p], back(p))

    def mu_copy(p):
        return copy(mu, mu_out.at[p], mu_ss.at[p], mu_rs.at[p], back(p))

    def z_copy(i):
        return copy(part, zbuf.at[grp], z_ss.at[i], z_rs.at[i], z_peer(i))

    def y_copy(i):
        own = coarse_out.at[box]
        return copy(own, own, y_ss.at[i], y_rs.at[i], y_peer(i))

    def x_copy(i):
        own = coarse_out.at[pl.ds(bx * 8, 8)]
        return copy(own, own, x_ss.at[i], x_rs.at[i], x_peer(i))

    def each(count, first, act):
        def one(i, c):
            act(i + first)
            return c

        lax.fori_loop(0, count, one, 0)

    each(SLOTS - 1, 0, lambda i: req_copy(slot_of(i)).start())
    each(3, 1, lambda i: z_copy(i).start())
    each(SLOTS - 1, 0, lambda i: mu_copy(slot_of(i)).start())

    left = iota((16, 128), 1) < 64

    turn(coupling, weights, 0, 6)
    asked_v[REACH] = jnp.zeros((1, 128), I32)
    each(SLOTS - 1, 0, lambda i: req_copy(slot_of(i)).wait_recv())
    local = pltpu.make_async_copy(asked_v, asked_s, loc_s.at[0])
    local.start()
    local.wait()

    def serve(i):
        p = slot_of(i)
        for q in range(ROOM // 2):
            a = leaf[asked_s[p, 0, 2 * q]]
            b = leaf[asked_s[p, 0, 2 * q + 1]]
            send[p, q * 16 : (q + 1) * 16, :] = jnp.where(left, a, b)
        leaf_copy(p).start()

    each(SLOTS - 1, 0, serve)

    zbuf[grp] = part[...]
    each(3, 1, lambda i: z_copy(i).wait())
    coarse_out[box] = (zbuf[0] + zbuf[1] + zbuf[2] + zbuf[3]).astype(BF)
    each(7, 1, lambda i: y_copy(i).start())
    turn(coupling, weights, 6, 36)
    each(7, 1, lambda i: y_copy(i).wait())
    each(3, 1, lambda i: x_copy(i).start())
    turn(coupling, weights, 36, 79)
    each(3, 1, lambda i: x_copy(i).wait())

    each(SLOTS - 1, 0, lambda i: req_copy(slot_of(i)).wait_send())
    each(SLOTS - 1, 0, lambda i: mu_copy(slot_of(i)).wait())
    each(SLOTS - 1, 0, lambda i: leaf_copy(slot_of(i)).wait())


def exchange(req, leaf_twice, mu, part, coupling):
    sem = pltpu.SemaphoreType.DMA
    return pl.pallas_call(
        exchange_kernel,
        out_shape=(
            jax.ShapeDtypeStruct((SLOTS, 256, 128), BF),
            jax.ShapeDtypeStruct((SLOTS, 144, 128), BF),
            jax.ShapeDtypeStruct((32, 16, 128), BF),
            jax.ShapeDtypeStruct((KINDS, 4, 32, 128), BF),
        ),
        in_specs=[VMEM] * 5,
        out_specs=[VMEM] * 4,
        scratch_shapes=[
            pltpu.VMEM((SLOTS, 1, 128), I32),
            pltpu.SMEM((SLOTS, 1, 128), I32),
            pltpu.VMEM((SLOTS, 256, 128), BF),
            pltpu.VMEM((4, 16, 128), F32),
        ]
        + [sem((SLOTS,))] * 7
        + [sem((8,))] * 6,
        compiler_params=pltpu.CompilerParams(
            collective_id=0, has_side_effects=True, vmem_limit_bytes=50 << 20
        ),
        name="exchange",
    )(req, leaf_twice, mu, part, coupling)


def far_kernel(
    rows_idx, kinds_idx, req, meta, own_leaf, own_mu, leaf_in, mu_in, coarse_in, weights, out, table
):
    l = iota((128, 512), 0)
    n = iota((128, 512), 1)
    spread = jnp.where(l == (n >> 7) * 32 + (n & 31), 1.0, 0.0).astype(BF)
    table[ZERO_ROW] = jnp.zeros((32, 128), BF)

    def fill(block, places):
        y = jnp.dot(block, spread, preferred_element_type=F32).astype(BF)
        for i, (a, b, h) in enumerate(places):
            s = slice(i * 16, (i + 1) * 16)
            first = [y[s, 0:128], y[s, 128:256]]
            table[a] = jnp.concatenate([first[h], first[1 - h]], axis=0)
            if b is not None:
                last = [y[s, 256:384], y[s, 384:512]]
                table[b] = jnp.concatenate([last[h], last[1 - h]], axis=0)

    def mu_places(p):
        mid = [(MID_ROW + p * 16 + 2 * i, MID_ROW + p * 16 + 2 * i + 1, 1) for i in range(8)]
        return mid + [(UPPER_ROW + p * 2, UPPER_ROW + p * 2 + 1, 0)]

    def peer(i, c):
        p = slot_of(i)
        fill(
            leaf_in[p],
            [
                (p * LEAFS + req[p, 0, 2 * q], p * LEAFS + req[p, 0, 2 * q + 1], 0)
                for q in range(16)
            ],
        )
        fill(mu_in[p], mu_places(p))
        return c

    lax.fori_loop(0, SLOTS - 1, peer, 0)
    fill(own_mu[...], mu_places(REACH))

    def own(i, c):
        base = REACH * LEAFS + i * 32
        fill(
            own_leaf[pl.ds(pl.multiple_of(i * 256, 256), 256), :],
            [(base + 2 * q, base + 2 * q + 1, 0) for q in range(16)],
        )
        return c

    lax.fori_loop(0, 4, own, 0)

    def coarse(i, c):
        fill(
            coarse_in[pl.ds(pl.multiple_of(i * 128, 128), 128), :],
            [(COARSE_ROW + i * 8 + q, None, 1) for q in range(8)],
        )
        return c

    lax.fori_loop(0, 4, coarse, 0)

    lane = iota((32, 128), 1)
    m1, m2, m3 = lane < 32, lane < 64, lane < 96
    left = iota((16, 128), 1) < 64

    def merge(a, b, c, d):
        return jnp.where(m2, jnp.where(m1, a, b), jnp.where(m3, c, d))

    def one(t, batches):
        acc = None
        for b in range(batches):
            cols, quads = [], []
            for g in range(2):
                base = b * 16 + g * 8
                cols.append(
                    jnp.concatenate([weights[kinds_idx[t * 256 + base + j]] for j in range(8)], axis=0)
                )
                quads.append(
                    jnp.concatenate(
                        [
                            merge(*[table[rows_idx[t * 256 + base + q * 4 + i]] for i in range(4)])
                            for q in range(2)
                        ],
                        axis=1,
                    )
                )
            d = jnp.dot(
                jnp.concatenate(quads, axis=0),
                jnp.concatenate(cols, axis=1),
                preferred_element_type=F32,
            )
            acc = d if acc is None else acc + d
        u = jnp.where(
            left, acc[0:16, 0:128] + acc[32:48, 128:256], acc[16:32, 0:128] + acc[48:64, 128:256]
        )
        out[t] = (u + pltpu.roll(u, 64, 1))[:, :64]

    def four(i, c, batches):
        for k in range(4):
            one(meta[0, i * 4 + k], batches)
        return c

    first = 0
    for batches in range(SLOT_PAD // 16, 5, -1):
        last = meta[1, batches - 1] if batches > 6 else TARGETS // 4
        lax.fori_loop(first, last, functools.partial(four, batches=batches), 0)
        first = last


def far(rows_idx, kinds_idx, req, meta, own_leaf, own_mu, leaf_in, mu_in, coarse_in, weights):
    return pl.pallas_call(
        far_kernel,
        out_shape=jax.ShapeDtypeStruct((TARGETS, 16, 64), F32),
        in_specs=[SMEM] * 4 + [VMEM] * 6,
        out_specs=VMEM,
        scratch_shapes=[pltpu.VMEM((TABLE_ROWS, 32, 128), BF)],
        compiler_params=pltpu.CompilerParams(vmem_limit_bytes=60 << 20),
        name="far",
    )(rows_idx, kinds_idx, req, meta, own_leaf, own_mu, leaf_in, mu_in, coarse_in, weights)


def pairs(blocks):
    n = blocks.shape[0]
    return blocks.reshape(n // 2, 2, 16, 64).transpose(0, 2, 1, 3).reshape(n * 8, 128)


def lift(matrices, children):
    terms = jnp.einsum("bpc,bvc->bvp", matrices, children, preferred_element_type=F32)
    return terms


def lower(matrices, parents, local):
    terms = jnp.einsum("bpc,bvp->bvc", matrices, parents, preferred_element_type=F32)
    return (local + terms).astype(BF)


def on_device(
    charges, leaf_basis, transfer0, transfer1, transfer2, coupling,
    lists0, lists1, lists2, lists3, kinds0, kinds1, kinds2, kinds3,
):
    member = lax.axis_index("grp")
    samples = charges.reshape(16, 128, 256)
    e0 = transfer0.reshape(128, 64, 64)
    e1 = transfer1.reshape(16, 64, 64)
    e2 = transfer2.reshape(2, 64, 64)
    leaf = jnp.einsum("bri,vbi->bvr", leaf_basis, samples, preferred_element_type=F32).astype(BF)
    mid = lift(e0, leaf).reshape(16, 8, 16, 64).sum(axis=1).astype(BF)
    upper = lift(e1, mid).reshape(2, 8, 16, 64).sum(axis=1).astype(BF)
    part = lift(e2, upper).sum(axis=0)
    part = jnp.concatenate([part, jnp.zeros((16, 64), F32)], axis=1)
    leaf_twice = jnp.concatenate([leaf, leaf], axis=2)
    own_leaf = pairs(leaf)
    own_mu = jnp.concatenate([pairs(mid), pairs(upper)], axis=0)

    rows_idx, kinds_idx, req, meta = plan(
        (lists0, lists1, lists2, lists3), (kinds0, kinds1, kinds2, kinds3)
    )
    by_kind = coupling.reshape(4, KINDS, 32, 128).transpose(1, 2, 0, 3).reshape(KINDS, 128, 128)
    leaf_in, mu_in, coarse_in, weights = exchange(req, leaf_twice, own_mu, part, by_kind)
    local = far(
        rows_idx.reshape(-1), kinds_idx.reshape(-1), req, meta, own_leaf, own_mu, leaf_in, mu_in,
        coarse_in.reshape(512, 128), weights.reshape(4 * KINDS, 32, 128),
    )
    leaf_local = local[0:128]
    mid_local = local[128:144]
    upper_local = local[144:146]
    coarse_field = local[146:147].astype(BF)
    upper_field = lower(e2, jnp.repeat(coarse_field, 2, axis=0), upper_local)
    mid_field = lower(e1, jnp.repeat(upper_field, 8, axis=0), mid_local)
    leaf_field = lower(e0, jnp.repeat(mid_field, 8, axis=0), leaf_local)
    potential = jnp.einsum("bri,bvr->vbi", leaf_basis, leaf_field, preferred_element_type=F32)
    return potential.astype(BF).reshape(16, 128 * 256)


def solution(mesh):
    both = ("boxes", "grp")
    in_specs = (
        P(None, both),
        P(both, None, None),
        P(both, None),
        P(both, None),
        P(both, None),
        P(),
        P(both, None),
        P(both, None),
        P(both, None),
        P("boxes", None),
        P(both, None),
        P(both, None),
        P(both, None),
        P("boxes", None),
    )
    return jax.shard_map(
        on_device, mesh=mesh, in_specs=in_specs, out_specs=P(None, both), check_vma=False
    )
```

```python
import functools

import jax
import jax.numpy as jnp
from jax import lax
from jax.experimental import pallas as pl
from jax.experimental.pallas import tpu as pltpu
from jax.sharding import PartitionSpec as P

BF = jnp.bfloat16
F32 = jnp.float32
I32 = jnp.int32
MESH = pl.DeviceIdType.MESH

DEV = 128
REACH = 13
SLOTS = 28
LEAFS = 128
ROOM = 32
SLOT_PAD = 192
TARGETS = 148
ZERO_ROW = SLOTS * LEAFS
MID_ROW = ZERO_ROW + 8
UPPER_ROW = MID_ROW + SLOTS * 16
COARSE_ROW = UPPER_ROW + SLOTS * 2
TABLE_ROWS = COARSE_ROW + 32
KINDS = 316
VMEM = pl.BlockSpec(memory_space=pltpu.VMEM)
ANY = pl.BlockSpec(memory_space=pl.ANY)
SMEM = pl.BlockSpec(memory_space=pltpu.SMEM)
TURN_PARTS = ((0, 10, 2), (10, 43, 3), (43, 79, 3))
NT = (((1,), (1,)), ((), ()))


def iota(shape, dim):
    return lax.broadcasted_iota(I32, shape, dim)


def plan_kernel(l0, l1, l2, l3, k0, k1, k2, k3, rows_flat, kinds_flat, req_out, meta, rows_out, kinds_out):
    me = lax.axis_index("boxes") * 4 + lax.axis_index("grp")
    rows_out[...] = jnp.full(rows_out.shape, ZERO_ROW, I32)
    kinds_out[...] = jnp.zeros(kinds_out.shape, I32)
    start = 0
    for level, (lists, kinds, count, offset) in enumerate(
        ((l0, k0, 128, 0), (l1, k1, 16, MID_ROW), (l2, k2, 2, UPPER_ROW))
    ):
        ids = lists[...]
        whole = DEV * count
        rel = lax.rem(ids - (me - REACH) * count + whole, whole)
        far = (REACH + DEV // 2) * count
        rel = jnp.where(rel >= far, rel - far + (SLOTS - 1) * count, rel)
        rows_out[start : start + count, 0:189] = jnp.where(ids >= 0, rel + offset, ZERO_ROW)
        kinds_out[start : start + count, 0:189] = kinds[...] * 4 + level
        start += count
    ids = l3[...]
    rows_out[start : start + 1, 0:189] = jnp.where(ids >= 0, ids + COARSE_ROW, ZERO_ROW)
    kinds_out[start : start + 1, 0:189] = k3[...] * 4 + 3
    for flat, tiled in ((rows_flat, rows_out), (kinds_flat, kinds_out)):
        flat[pl.ds(0, TARGETS, stride=2), :] = tiled[:, 0:128]
        flat[pl.ds(1, TARGETS, stride=2), 0 : SLOT_PAD - 128] = tiled[:, 128:SLOT_PAD]

    live = jnp.where(rows_out[...] != ZERO_ROW, 1.0, 0.0).astype(BF)
    down = jnp.dot(live, jnp.ones((SLOT_PAD, 256), BF), preferred_element_type=F32)[:, :TARGETS]
    across = lax.dot_general(jnp.ones((8, SLOT_PAD), BF), live, NT, preferred_element_type=F32)
    down = (down.astype(I32) + 15) >> 4
    across = (across[0:1].astype(I32) + 15) >> 4
    t_down, t_across = iota((TARGETS, TARGETS), 0), iota((TARGETS, TARGETS), 1)
    before = (across > down) | ((across == down) & (t_across < t_down))
    place = jnp.sum(jnp.where(before, 1.0, 0.0), axis=1, keepdims=True)
    here = place == t_across.astype(F32)
    order = jnp.sum(jnp.where(here, t_down.astype(F32), 0.0), axis=0, keepdims=True).astype(I32)
    meta[...] = jnp.zeros(meta.shape, I32)
    meta[0:1, 0:TARGETS] = order
    sub = iota((16, TARGETS), 0)
    over = jnp.sum(jnp.where(across > sub, 1.0, 0.0), axis=1, keepdims=True).astype(I32)
    ends = jnp.where(iota((16, 256), 1) == iota((16, 256), 0), (over + 3) >> 2, 0)
    meta[1:2, :] = jnp.sum(ends, axis=0, keepdims=True)

    sub_lo = iota((LEAFS, SLOT_PAD), 0)
    sub_hi = iota((32, SLOT_PAD), 0)

    def mark(t, seen):
        row = rows_out[pl.ds(t, 1), :]
        lo = jnp.where(sub_lo == (row & 127), 1.0, 0.0).astype(BF)
        hi = jnp.where(sub_hi == (row >> 7), 1.0, 0.0).astype(BF)
        return seen + lax.dot_general(hi, lo, NT, preferred_element_type=F32)

    seen = lax.fori_loop(0, LEAFS, mark, jnp.zeros((32, LEAFS), F32), unroll=4)
    needed = seen > 0.5
    lane = iota((32, LEAFS), 1)
    upto = (
        iota((LEAFS, LEAFS), 0) <= iota((LEAFS, LEAFS), 1)
    )
    rank = jnp.dot(
        jnp.where(needed, 1.0, 0.0).astype(BF),
        jnp.where(upto, 1.0, 0.0).astype(BF),
        preferred_element_type=F32,
    )
    rank = jnp.where(needed, rank, 0.0)
    lane_f = lane.astype(F32)
    asked = jnp.zeros((32, LEAFS), F32)
    for q in range(ROOM):
        pick = jnp.sum(jnp.where(rank == q + 1.0, lane_f, 0.0), axis=1, keepdims=True)
        asked = jnp.where(lane == q, pick, asked)
    asked = asked.astype(I32)
    for h in range(SLOTS):
        req_out[h] = asked[h : h + 1, :]


def plan(lists, kinds):
    return pl.pallas_call(
        plan_kernel,
        out_shape=(
            jax.ShapeDtypeStruct((2 * TARGETS, 128), I32),
            jax.ShapeDtypeStruct((2 * TARGETS, 128), I32),
            jax.ShapeDtypeStruct((SLOTS, 1, 128), I32),
            jax.ShapeDtypeStruct((8, 256), I32),
        ),
        in_specs=[VMEM] * 8,
        out_specs=[VMEM] * 4,
        scratch_shapes=[pltpu.VMEM((TARGETS, SLOT_PAD), I32)] * 2,
        compiler_params=pltpu.CompilerParams(vmem_limit_bytes=32 << 20),
        name="plan",
    )(*lists, *kinds)


def left_half():
    return iota((16, 128), 1) < 64


def lift(children, matrices):
    left = left_half()
    zero = jnp.zeros((16, 128), BF)
    rows = [
        jnp.concatenate([jnp.where(left, m, zero), jnp.where(left, zero, m)], axis=0)
        for m in children
    ]
    return lax.dot_general(
        jnp.concatenate(rows, axis=1),
        jnp.concatenate(matrices, axis=1),
        NT,
        preferred_element_type=F32,
    )


def weave(split):
    lane = iota((32, 128), 1) & 63
    total = None
    for h in range(2):
        put = jnp.where(lane == 2 * iota((32, 128), 0) + h, 1.0, 0.0).astype(BF)
        part = jnp.dot(split[h * 16 : (h + 1) * 16], put, preferred_element_type=F32)
        total = part if total is None else total + part
    return total.astype(BF)


def unweave(block):
    parts = []
    for h in range(2):
        row, lane = iota((128, 32), 0), iota((128, 32), 1)
        put = jnp.where(row == 2 * lane + h, 1.0, 0.0).astype(BF)
        parts.append(jnp.dot(block, put, preferred_element_type=F32))
    return jnp.concatenate(parts, axis=0).astype(BF)


def lowered(parent, matrix, local):
    o = jnp.dot(parent, matrix, preferred_element_type=F32)
    u = jnp.where(left_half(), o[0:16], o[16:32])
    return (local + (u + pltpu.roll(u, 64, 1))).astype(BF)


def turn(coupling, weights, first, last, per):
    eye = jnp.where(iota((128, 128), 0) == iota((128, 128), 1), 1.0, 0.0).astype(BF)
    row, col = iota((256, 256), 0), iota((256, 256), 1)
    fits = (col & 63) == 2 * ((row & 127) >> 2) + (row >> 7)
    pick = [
        jnp.where(fits & (((col >> 6) ^ h) == (row & 3)), 1.0, 0.0).astype(BF) for h in range(2)
    ]
    left = iota((32, 128), 1) < 64

    def group(i):
        rows = [[], []]
        for j in range(2):
            pair = coupling[pl.ds(i * 4 + 2 * j, 2)].reshape(256, 128)
            t = lax.dot_general(eye, pair, NT, preferred_element_type=F32).astype(BF)
            for k in range(2):
                y = t[:, k * 128 : (k + 1) * 128]
                for h in range(2):
                    a = y[h * 32 : h * 32 + 32]
                    b = y[64 + h * 32 : 64 + h * 32 + 32]
                    rows[h].append(jnp.concatenate([a, b], axis=1))
        half = [
            jnp.dot(jnp.concatenate(rows[h], axis=0), pick[h], preferred_element_type=F32).astype(BF)
            for h in range(2)
        ]
        for k in range(4):
            for p in range(2):
                a = half[0][k * 32 : k * 32 + 32, p * 128 : (p + 1) * 128]
                b = half[1][k * 32 : k * 32 + 32, p * 128 : (p + 1) * 128]
                weights[i * 4 + k, 2 * p] = jnp.where(left, a, b)
                weights[i * 4 + k, 2 * p + 1] = jnp.where(left, b, a)

    def step(i, c):
        for k in range(per):
            group(first + i * per + k)
        return c

    lax.fori_loop(0, (last - first) // per, step, 0)


def slot_of(i):
    return i + (i + 15) // 28


def offset_of(p):
    return p - REACH + (DEV // 2 - SLOTS + 1 + REACH) * (p // (SLOTS - 1))


def exchange_kernel(
    req, charges_any, basis_any, transfer, coupling_any,
    leaf_out, mu_out, coarse_out, own_leaf, weights_any,
    asked_v, asked_s, send, zbuf, coupling, weights, in_s, out_s,
    charges, basis, leaf, mid, part,
    req_ss, req_rs, loc_s, leaf_ss, leaf_rs, mu_ss, mu_rs, z_ss, z_rs, y_ss, y_rs, x_ss, x_rs,
):
    box = lax.axis_index("boxes")
    grp = lax.axis_index("grp")
    me = box * 4 + grp
    bx = box // 8
    by = box % 8

    def there(p):
        t = (me + offset_of(p) + DEV) % DEV
        return (t // 4, t % 4)

    def back(p):
        t = (me - offset_of(p) + DEV) % DEV
        return (t // 4, t % 4)

    def z_peer(i):
        return (box, (grp + i) % 4)

    def y_peer(i):
        return (bx * 8 + (by + i) % 8, grp)

    def x_peer(i):
        return (((bx + i) % 4) * 8 + by, grp)

    loads = [
        pltpu.make_async_copy(charges_any, charges, in_s.at[0]),
        pltpu.make_async_copy(basis_any, basis, in_s.at[1]),
        pltpu.make_async_copy(coupling_any, coupling, in_s.at[2]),
    ]
    for load in loads:
        load.start()
    barrier = pltpu.get_barrier_semaphore()

    def greet(to, first, count):
        def one(i, c):
            pl.semaphore_signal(barrier, inc=1, device_id=to(i + first), device_id_type=MESH)
            return c

        lax.fori_loop(0, count, one, 0)

    greet(lambda i: there(slot_of(i)), 0, SLOTS - 1)
    greet(z_peer, 1, 3)
    greet(y_peer, 1, 7)
    greet(x_peer, 1, 3)
    pl.semaphore_wait(barrier, SLOTS - 1 + 13)

    def copy(src, dst, ss, rs, to):
        return pltpu.make_async_remote_copy(
            src_ref=src, dst_ref=dst, send_sem=ss, recv_sem=rs, device_id=to, device_id_type=MESH
        )

    def req_copy(p):
        return copy(req.at[p], asked_v.at[p], req_ss.at[p], req_rs.at[p], there(p))

    def leaf_copy(p):
        return copy(send.at[p], leaf_out.at[p], leaf_ss.at[p], leaf_rs.at[p], back(p))

    def mu_copy(p):
        return copy(mu_out.at[REACH], mu_out.at[p], mu_ss.at[p], mu_rs.at[p], back(p))

    def z_copy(i):
        return copy(part, zbuf.at[grp], z_ss.at[i], z_rs.at[i], z_peer(i))

    def y_copy(i):
        own = coarse_out.at[box]
        return copy(own, own, y_ss.at[i], y_rs.at[i], y_peer(i))

    def x_copy(i):
        own = coarse_out.at[pl.ds(bx * 8, 8)]
        return copy(own, own, x_ss.at[i], x_rs.at[i], x_peer(i))

    def each(count, first, act):
        def one(i, c):
            act(i + first)
            return c

        lax.fori_loop(0, count, one, 0)

    each(SLOTS - 1, 0, lambda i: req_copy(slot_of(i)).start())
    left = left_half()
    loads[0].wait()
    loads[1].wait()

    def boxes(i, c):
        blocks = []
        for k in range(8):
            b = i * 8 + k
            w = basis[b]
            points = charges[:, pl.ds(pl.multiple_of(b * 256, 256), 256)]
            m = lax.dot_general(
                points, jnp.concatenate([w, w], axis=0), NT, preferred_element_type=F32
            ).astype(BF)
            leaf[b] = m
            blocks.append(m)
        for k in range(4):
            place = pl.ds(pl.multiple_of((i * 4 + k) * 16, 16), 16)
            own_leaf[place, :] = jnp.where(left, blocks[2 * k], blocks[2 * k + 1])
        return c

    lax.fori_loop(0, LEAFS // 8, boxes, 0)


    def turn_part(k):
        first, last, per = TURN_PARTS[k]
        turn(coupling, weights, first, last, per)
        store_part(k).start()

    def store_part(k):
        span = pl.ds(TURN_PARTS[k][0] * 4, (TURN_PARTS[k][1] - TURN_PARTS[k][0]) * 4)
        return pltpu.make_async_copy(weights.at[span], weights_any.at[span], out_s.at[k])

    asked_v[REACH] = jnp.zeros((1, 128), I32)
    each(SLOTS - 1, 0, lambda i: req_copy(slot_of(i)).wait_recv())
    local = pltpu.make_async_copy(asked_v, asked_s, loc_s.at[0])
    local.start()
    local.wait()

    def serve(i):
        p = slot_of(i)
        for q in range(ROOM // 2):
            a = leaf[asked_s[p, 0, 2 * q]]
            b = leaf[asked_s[p, 0, 2 * q + 1]]
            send[p, q * 16 : (q + 1) * 16, :] = jnp.where(left, a, b)
        leaf_copy(p).start()

    each(SLOTS - 1, 0, serve)

    def mids(i, c):
        for k in range(4):
            t = i * 4 + k
            mid[t] = weave(
                lift([leaf[t * 8 + j] for j in range(8)], [transfer[t * 8 + j] for j in range(8)])
                .astype(BF)
            )
        return c

    lax.fori_loop(0, 4, mids, 0)
    for q in range(8):
        mu_out[REACH, q * 16 : (q + 1) * 16, :] = jnp.where(left, mid[2 * q], mid[2 * q + 1])
    upper = []
    for t in range(2):
        children = range(t * 8, t * 8 + 8)
        sums = lift([mid[j] for j in children], [transfer[128 + j] for j in children])
        upper.append(weave(sums.astype(BF)))
    mu_out[REACH, 128:144, :] = jnp.where(left, upper[0], upper[1])
    part[...] = jnp.zeros(part.shape, F32)
    part[:, 0:32] = lift(upper, [transfer[144], transfer[145]])
    zbuf[grp] = part[...]
    each(3, 1, lambda i: z_copy(i).start())
    each(SLOTS - 1, 0, lambda i: mu_copy(slot_of(i)).start())
    loads[2].wait()
    turn_part(0)
    each(3, 1, lambda i: z_copy(i).wait())
    whole = (zbuf[0] + zbuf[1] + zbuf[2] + zbuf[3]).astype(BF)
    coarse_out[box] = weave(whole[:, 0:32])
    each(7, 1, lambda i: y_copy(i).start())
    turn_part(1)
    each(7, 1, lambda i: y_copy(i).wait())
    each(3, 1, lambda i: x_copy(i).start())
    turn_part(2)
    each(3, 1, lambda i: x_copy(i).wait())

    each(SLOTS - 1, 0, lambda i: req_copy(slot_of(i)).wait_send())
    each(SLOTS - 1, 0, lambda i: mu_copy(slot_of(i)).wait())
    each(SLOTS - 1, 0, lambda i: leaf_copy(slot_of(i)).wait())
    for k in range(len(TURN_PARTS)):
        store_part(k).wait()


def exchange(req, charges, basis, transfer, coupling):
    sem = pltpu.SemaphoreType.DMA
    return pl.pallas_call(
        exchange_kernel,
        out_shape=(
            jax.ShapeDtypeStruct((SLOTS, 256, 128), BF),
            jax.ShapeDtypeStruct((SLOTS, 144, 128), BF),
            jax.ShapeDtypeStruct((32, 16, 128), BF),
            jax.ShapeDtypeStruct((1024, 128), BF),
            jax.ShapeDtypeStruct((KINDS, 4, 32, 128), BF),
        ),
        in_specs=[VMEM, ANY, ANY, VMEM, ANY],
        out_specs=[VMEM] * 4 + [ANY],
        scratch_shapes=[
            pltpu.VMEM((SLOTS, 1, 128), I32),
            pltpu.SMEM((SLOTS, 1, 128), I32),
            pltpu.VMEM((SLOTS, 256, 128), BF),
            pltpu.VMEM((4, 32, 128), F32),
            pltpu.VMEM((KINDS, 128, 128), BF),
            pltpu.VMEM((KINDS, 4, 32, 128), BF),
            sem((3,)),
            sem((len(TURN_PARTS),)),
            pltpu.VMEM((16, 32768), BF),
            pltpu.VMEM((LEAFS, 64, 256), BF),
            pltpu.VMEM((LEAFS, 16, 128), BF),
            pltpu.VMEM((16, 16, 128), BF),
            pltpu.VMEM((32, 128), F32),
        ]
        + [sem((SLOTS,))] * 7
        + [sem((8,))] * 6,
        compiler_params=pltpu.CompilerParams(
            collective_id=0, has_side_effects=True, vmem_limit_bytes=50 << 20
        ),
        name="exchange",
    )(req, charges, basis, transfer, coupling)


def far_kernel(
    rows_idx, kinds_idx, req, meta, own_leaf, leaf_in, mu_in, coarse_in, transfer,
    weights_any, basis_any, out,
    table, weights, basis, local, parents, in_s,
):
    load = pltpu.make_async_copy(weights_any, weights, in_s.at[0])
    load_basis = pltpu.make_async_copy(basis_any, basis, in_s.at[1])
    load.start()
    load_basis.start()
    l = iota((128, 512), 0)
    n = iota((128, 512), 1)
    spread = jnp.where(l == (n >> 7) * 32 + (n & 31), 1.0, 0.0).astype(BF)
    table[ZERO_ROW] = jnp.zeros((32, 128), BF)

    def fill(block, places):
        y = jnp.dot(block, spread, preferred_element_type=F32).astype(BF)
        for i, (a, b, h) in enumerate(places):
            s = slice(i * 16, (i + 1) * 16)
            first = [y[s, 0:128], y[s, 128:256]]
            table[a] = jnp.concatenate([first[h], first[1 - h]], axis=0)
            if b is not None:
                last = [y[s, 256:384], y[s, 384:512]]
                table[b] = jnp.concatenate([last[h], last[1 - h]], axis=0)

    def mu_places(p):
        mid = [(MID_ROW + p * 16 + 2 * i, MID_ROW + p * 16 + 2 * i + 1, 1) for i in range(8)]
        return mid + [(UPPER_ROW + p * 2, UPPER_ROW + p * 2 + 1, 0)]

    def peers(i, c):
        for k in range(3):
            peer(i * 3 + k)
        return c

    def peer(i):
        p = slot_of(i)
        fill(
            leaf_in[p],
            [
                (p * LEAFS + req[p, 0, 2 * q], p * LEAFS + req[p, 0, 2 * q + 1], 0)
                for q in range(16)
            ],
        )
        fill(mu_in[p], mu_places(p))

    lax.fori_loop(0, (SLOTS - 1) // 3, peers, 0)
    fill(mu_in[REACH], mu_places(REACH))

    def own(i, c):
        base = REACH * LEAFS + i * 32
        fill(
            own_leaf[pl.ds(pl.multiple_of(i * 256, 256), 256), :],
            [(base + 2 * q, base + 2 * q + 1, 0) for q in range(16)],
        )
        return c

    lax.fori_loop(0, 4, own, 0)

    def coarse(i, c):
        fill(
            coarse_in[pl.ds(pl.multiple_of(i * 128, 128), 128), :],
            [(COARSE_ROW + i * 8 + q, None, 1) for q in range(8)],
        )
        return c

    lax.fori_loop(0, 4, coarse, 0)

    load.wait()
    lane = iota((32, 128), 1)
    m1, m2, m3 = lane < 32, lane < 64, lane < 96
    left = iota((16, 128), 1) < 64

    def merge(a, b, c, d):
        return jnp.where(m2, jnp.where(m1, a, b), jnp.where(m3, c, d))

    def one(t, batches):
        acc = None
        for b in range(batches):
            cols, quads = [], []
            for g in range(2):
                base = b * 16 + g * 8
                cols.append(
                    jnp.concatenate([weights[kinds_idx[t * 256 + base + j]] for j in range(8)], axis=0)
                )
                quads.append(
                    jnp.concatenate(
                        [
                            merge(*[table[rows_idx[t * 256 + base + q * 4 + i]] for i in range(4)])
                            for q in range(2)
                        ],
                        axis=1,
                    )
                )
            d = jnp.dot(
                jnp.concatenate(quads, axis=0),
                jnp.concatenate(cols, axis=1),
                preferred_element_type=F32,
            )
            acc = d if acc is None else acc + d
        u = jnp.where(
            left, acc[0:16, 0:128] + acc[32:48, 128:256], acc[16:32, 0:128] + acc[48:64, 128:256]
        )
        local[t] = u + pltpu.roll(u, 64, 1)

    def four(i, c, batches):
        for k in range(4):
            one(meta[0, i * 4 + k], batches)
        return c

    first = 0
    for batches in range(SLOT_PAD // 16, 5, -1):
        last = meta[1, batches - 1] if batches > 6 else TARGETS // 4
        lax.fori_loop(first, last, functools.partial(four, batches=batches), 0)
        first = last

    load_basis.wait()
    coarse_field = unweave(local[146].astype(BF))
    for u in range(2):
        upper_field = unweave(lowered(coarse_field, transfer[144 + u], local[144 + u]))
        for m in range(u * 8, u * 8 + 8):
            parents[m] = unweave(lowered(upper_field, transfer[128 + m], local[128 + m]))

    def boxes(m, c):
        parent = parents[m]
        for j in range(8):
            b = m * 8 + j
            field = lowered(parent, transfer[b], local[b])
            points = jnp.dot(field[:, :64], basis[b], preferred_element_type=F32)
            out[:, pl.ds(pl.multiple_of(b * 256, 256), 256)] = points.astype(BF)
        return c

    lax.fori_loop(0, 16, boxes, 0)


def far(rows_idx, kinds_idx, req, meta, own_leaf, leaf_in, mu_in, coarse_in, transfer, weights, basis):
    return pl.pallas_call(
        far_kernel,
        out_shape=jax.ShapeDtypeStruct((16, LEAFS * 256), BF),
        in_specs=[SMEM] * 4 + [VMEM] * 5 + [ANY] * 2,
        out_specs=VMEM,
        scratch_shapes=[
            pltpu.VMEM((TABLE_ROWS, 32, 128), BF),
            pltpu.VMEM((4 * KINDS, 32, 128), BF),
            pltpu.VMEM((LEAFS, 64, 256), BF),
            pltpu.VMEM((TARGETS, 16, 128), F32),
            pltpu.VMEM((16, 32, 32), BF),
            pltpu.SemaphoreType.DMA((2,)),
        ],
        compiler_params=pltpu.CompilerParams(vmem_limit_bytes=60 << 20),
        name="far",
    )(
        rows_idx, kinds_idx, req, meta, own_leaf, leaf_in, mu_in, coarse_in, transfer, weights, basis
    )


def on_device(
    charges, leaf_basis, transfer0, transfer1, transfer2, coupling,
    lists0, lists1, lists2, lists3, kinds0, kinds1, kinds2, kinds3,
):
    transfer = jnp.concatenate([transfer0, transfer1, transfer2], axis=0).reshape(146, 32, 128)
    by_kind = coupling.reshape(4, KINDS, 32, 128).transpose(1, 2, 0, 3).reshape(KINDS, 128, 128)
    rows_idx, kinds_idx, req, meta = plan(
        (lists0, lists1, lists2, lists3), (kinds0, kinds1, kinds2, kinds3)
    )
    leaf_in, mu_in, coarse_in, own_leaf, weights = exchange(
        req, charges, leaf_basis, transfer, by_kind
    )
    return far(
        rows_idx.reshape(-1), kinds_idx.reshape(-1), req, meta, own_leaf, leaf_in, mu_in,
        coarse_in.reshape(512, 128), transfer, weights.reshape(4 * KINDS, 32, 128), leaf_basis,
    )


def solution(mesh):
    both = ("boxes", "grp")
    in_specs = (
        P(None, both),
        P(both, None, None),
        P(both, None),
        P(both, None),
        P(both, None),
        P(),
        P(both, None),
        P(both, None),
        P(both, None),
        P("boxes", None),
        P(both, None),
        P(both, None),
        P(both, None),
        P("boxes", None),
    )
    return jax.shard_map(
        on_device, mesh=mesh, in_specs=in_specs, out_specs=P(None, both), check_vma=False
    )
```

```python
import functools

import jax
import jax.numpy as jnp
from jax import lax
from jax.experimental import pallas as pl
from jax.experimental.pallas import tpu as pltpu
from jax.sharding import PartitionSpec as P

BF = jnp.bfloat16
F32 = jnp.float32
I32 = jnp.int32
MESH = pl.DeviceIdType.MESH

DEV = 128
REACH = 13
SLOTS = 28
LEAFS = 128
ROOM = 32
SLOT_PAD = 192
TARGETS = 148
ZERO_ROW = SLOTS * LEAFS
MID_ROW = ZERO_ROW + 8
UPPER_ROW = MID_ROW + SLOTS * 16
COARSE_ROW = UPPER_ROW + SLOTS * 2
TABLE_ROWS = COARSE_ROW + 32
KINDS = 316
VMEM = pl.BlockSpec(memory_space=pltpu.VMEM)
ANY = pl.BlockSpec(memory_space=pl.ANY)
SMEM = pl.BlockSpec(memory_space=pltpu.SMEM)
TURN_PARTS = ((0, 10, 2), (10, 43, 3), (43, 79, 3))
NT = (((1,), (1,)), ((), ()))


def iota(shape, dim):
    return lax.broadcasted_iota(I32, shape, dim)


def plan_kernel(
    l0, k0, l1_any, l2_any, l3_any, k1_any, k2_any, k3_any,
    rows_flat, kinds_flat, req_out, meta,
    rows_out, kinds_out, l1, l2, l3, k1, k2, k3, in_s,
):
    loads = [
        pltpu.make_async_copy(src, dst, in_s.at[i])
        for i, (src, dst) in enumerate(
            ((l1_any, l1), (l2_any, l2), (l3_any, l3), (k1_any, k1), (k2_any, k2), (k3_any, k3))
        )
    ]
    for load in loads:
        load.start()
    for load in loads:
        load.wait()
    me = lax.axis_index("boxes") * 4 + lax.axis_index("grp")
    rows_out[...] = jnp.full(rows_out.shape, ZERO_ROW, I32)
    kinds_out[...] = jnp.zeros(kinds_out.shape, I32)
    start = 0
    for level, (lists, kinds, count, offset) in enumerate(
        ((l0, k0, 128, 0), (l1, k1, 16, MID_ROW), (l2, k2, 2, UPPER_ROW))
    ):
        ids = lists[...]
        whole = DEV * count
        rel = lax.rem(ids - (me - REACH) * count + whole, whole)
        far = (REACH + DEV // 2) * count
        rel = jnp.where(rel >= far, rel - far + (SLOTS - 1) * count, rel)
        rows_out[start : start + count, 0:189] = jnp.where(ids >= 0, rel + offset, ZERO_ROW)
        kinds_out[start : start + count, 0:189] = kinds[...] * 4 + level
        start += count
    ids = l3[...]
    rows_out[start : start + 1, 0:189] = jnp.where(ids >= 0, ids + COARSE_ROW, ZERO_ROW)
    kinds_out[start : start + 1, 0:189] = k3[...] * 4 + 3
    for flat, tiled in ((rows_flat, rows_out), (kinds_flat, kinds_out)):
        flat[pl.ds(0, TARGETS, stride=2), :] = tiled[:, 0:128]
        flat[pl.ds(1, TARGETS, stride=2), 0 : SLOT_PAD - 128] = tiled[:, 128:SLOT_PAD]

    live = jnp.where(rows_out[...] != ZERO_ROW, 1.0, 0.0).astype(BF)
    down = jnp.dot(live, jnp.ones((SLOT_PAD, 256), BF), preferred_element_type=F32)[:, :TARGETS]
    across = lax.dot_general(jnp.ones((8, SLOT_PAD), BF), live, NT, preferred_element_type=F32)
    down = (down.astype(I32) + 15) >> 4
    across = (across[0:1].astype(I32) + 15) >> 4
    t_down, t_across = iota((TARGETS, TARGETS), 0), iota((TARGETS, TARGETS), 1)
    before = (across > down) | ((across == down) & (t_across < t_down))
    place = jnp.sum(jnp.where(before, 1.0, 0.0), axis=1, keepdims=True)
    here = place == t_across.astype(F32)
    order = jnp.sum(jnp.where(here, t_down.astype(F32), 0.0), axis=0, keepdims=True).astype(I32)
    meta[...] = jnp.zeros(meta.shape, I32)
    meta[0:1, 0:TARGETS] = order
    sub = iota((16, TARGETS), 0)
    over = jnp.sum(jnp.where(across > sub, 1.0, 0.0), axis=1, keepdims=True).astype(I32)
    ends = jnp.where(iota((16, 256), 1) == iota((16, 256), 0), (over + 3) >> 2, 0)
    meta[1:2, :] = jnp.sum(ends, axis=0, keepdims=True)

    sub_lo = iota((LEAFS, SLOT_PAD), 0)
    sub_hi = iota((32, SLOT_PAD), 0)

    def mark(t, seen):
        row = rows_out[pl.ds(t, 1), :]
        lo = jnp.where(sub_lo == (row & 127), 1.0, 0.0).astype(BF)
        hi = jnp.where(sub_hi == (row >> 7), 1.0, 0.0).astype(BF)
        return seen + lax.dot_general(hi, lo, NT, preferred_element_type=F32)

    seen = lax.fori_loop(0, LEAFS, mark, jnp.zeros((32, LEAFS), F32), unroll=4)
    needed = seen > 0.5
    lane = iota((32, LEAFS), 1)
    upto = (
        iota((LEAFS, LEAFS), 0) <= iota((LEAFS, LEAFS), 1)
    )
    rank = jnp.dot(
        jnp.where(needed, 1.0, 0.0).astype(BF),
        jnp.where(upto, 1.0, 0.0).astype(BF),
        preferred_element_type=F32,
    )
    rank = jnp.where(needed, rank, 0.0)
    lane_f = lane.astype(F32)
    asked = jnp.zeros((32, LEAFS), F32)
    for q in range(ROOM):
        pick = jnp.sum(jnp.where(rank == q + 1.0, lane_f, 0.0), axis=1, keepdims=True)
        asked = jnp.where(lane == q, pick, asked)
    asked = asked.astype(I32)
    for h in range(SLOTS):
        req_out[h] = asked[h : h + 1, :]


def plan(lists, kinds):
    return pl.pallas_call(
        plan_kernel,
        out_shape=(
            jax.ShapeDtypeStruct((2 * TARGETS, 128), I32),
            jax.ShapeDtypeStruct((2 * TARGETS, 128), I32),
            jax.ShapeDtypeStruct((SLOTS, 1, 128), I32),
            jax.ShapeDtypeStruct((8, 256), I32),
        ),
        in_specs=[VMEM] * 2 + [ANY] * 6,
        out_specs=[VMEM] * 4,
        scratch_shapes=[pltpu.VMEM((TARGETS, SLOT_PAD), I32)] * 2
        + [pltpu.VMEM((n, 189), I32) for n in (16, 2, 1)] * 2
        + [pltpu.SemaphoreType.DMA((6,))],
        compiler_params=pltpu.CompilerParams(vmem_limit_bytes=60 << 20),
        name="plan",
    )(lists[0], kinds[0], *lists[1:], *kinds[1:])


def left_half():
    return iota((16, 128), 1) < 64


def lift(children, matrices):
    left = left_half()
    zero = jnp.zeros((16, 128), BF)
    rows = [
        jnp.concatenate([jnp.where(left, m, zero), jnp.where(left, zero, m)], axis=0)
        for m in children
    ]
    return lax.dot_general(
        jnp.concatenate(rows, axis=1),
        jnp.concatenate(matrices, axis=1),
        NT,
        preferred_element_type=F32,
    )


def weave(splits):
    lane = iota((32, 128), 1) & 63
    total = None
    for h in range(2):
        put = jnp.where(lane == 2 * iota((32, 128), 0) + h, 1.0, 0.0).astype(BF)
        rows = jnp.concatenate([x[h * 16 : (h + 1) * 16] for x in splits], axis=0)
        part = jnp.dot(rows, put, preferred_element_type=F32)
        total = part if total is None else total + part
    return total.astype(BF)


def unweave(blocks):
    x = jnp.concatenate(blocks, axis=0)
    parts = []
    for h in range(2):
        put = jnp.where(iota((128, 32), 0) == 2 * iota((128, 32), 1) + h, 1.0, 0.0).astype(BF)
        parts.append(jnp.dot(x, put, preferred_element_type=F32))
    return [
        jnp.concatenate([p[i * 16 : (i + 1) * 16] for p in parts], axis=0).astype(BF)
        for i in range(len(blocks))
    ]


def lowered(parent, matrices, locals_):
    left = left_half()
    o = jnp.dot(parent, jnp.concatenate(matrices, axis=1), preferred_element_type=F32)
    fields = []
    for i, local in enumerate(locals_):
        e = o[:, i * 128 : (i + 1) * 128]
        u = jnp.where(left, e[0:16], e[16:32])
        fields.append((local + (u + pltpu.roll(u, 64, 1))).astype(BF))
    return fields


def turn(coupling, weights, first, last, per):
    eye = jnp.where(iota((128, 128), 0) == iota((128, 128), 1), 1.0, 0.0).astype(BF)
    row, col = iota((256, 256), 0), iota((256, 256), 1)
    fits = (col & 63) == 2 * ((row & 127) >> 2) + (row >> 7)
    pick = [
        jnp.where(fits & (((col >> 6) ^ h) == (row & 3)), 1.0, 0.0).astype(BF) for h in range(2)
    ]
    left = iota((32, 128), 1) < 64

    def step(i, c):
        base = (first + i * per) * 4
        rows = [[], []]
        for j in range(2 * per):
            pair = coupling[pl.ds(base + 2 * j, 2)].reshape(256, 128)
            t = lax.dot_general(eye, pair, NT, preferred_element_type=F32).astype(BF)
            for k in range(2):
                y = t[:, k * 128 : (k + 1) * 128]
                for h in range(2):
                    a = y[h * 32 : h * 32 + 32]
                    b = y[64 + h * 32 : 64 + h * 32 + 32]
                    rows[h].append(jnp.concatenate([a, b], axis=1))
        half = [
            jnp.dot(jnp.concatenate(rows[h], axis=0), pick[h], preferred_element_type=F32).astype(BF)
            for h in range(2)
        ]
        for k in range(4 * per):
            for p in range(2):
                a = half[0][k * 32 : k * 32 + 32, p * 128 : (p + 1) * 128]
                b = half[1][k * 32 : k * 32 + 32, p * 128 : (p + 1) * 128]
                weights[base + k, 2 * p] = jnp.where(left, a, b)
                weights[base + k, 2 * p + 1] = jnp.where(left, b, a)
        return c

    lax.fori_loop(0, (last - first) // per, step, 0)


def slot_of(i):
    return i + (i + 15) // 28


def offset_of(p):
    return p - REACH + (DEV // 2 - SLOTS + 1 + REACH) * (p // (SLOTS - 1))


def exchange_kernel(
    req, charges_any, basis_any, transfer, coupling_any,
    leaf_out, mu_out, coarse_out, own_leaf, weights_any,
    asked_v, asked_s, send, zbuf, coupling, weights, in_s, out_s,
    charges, basis, leaf, split, mid, part,
    req_ss, req_rs, loc_s, leaf_ss, leaf_rs, mu_ss, mu_rs, z_ss, z_rs, y_ss, y_rs, x_ss, x_rs,
):
    box = lax.axis_index("boxes")
    grp = lax.axis_index("grp")
    me = box * 4 + grp
    bx = box // 8
    by = box % 8

    def there(p):
        t = (me + offset_of(p) + DEV) % DEV
        return (t // 4, t % 4)

    def back(p):
        t = (me - offset_of(p) + DEV) % DEV
        return (t // 4, t % 4)

    def z_peer(i):
        return (box, (grp + i) % 4)

    def y_peer(i):
        return (bx * 8 + (by + i) % 8, grp)

    def x_peer(i):
        return (((bx + i) % 4) * 8 + by, grp)

    loads = [
        pltpu.make_async_copy(charges_any, charges, in_s.at[0]),
        pltpu.make_async_copy(basis_any, basis, in_s.at[1]),
        pltpu.make_async_copy(coupling_any, coupling, in_s.at[2]),
    ]
    for load in loads:
        load.start()
    barrier = pltpu.get_barrier_semaphore()

    def greet(to, first, count):
        def one(i, c):
            pl.semaphore_signal(barrier, inc=1, device_id=to(i + first), device_id_type=MESH)
            return c

        lax.fori_loop(0, count, one, 0)

    greet(lambda i: there(slot_of(i)), 0, SLOTS - 1)
    greet(z_peer, 1, 3)
    greet(y_peer, 1, 7)
    greet(x_peer, 1, 3)
    pl.semaphore_wait(barrier, SLOTS - 1 + 13)

    def copy(src, dst, ss, rs, to):
        return pltpu.make_async_remote_copy(
            src_ref=src, dst_ref=dst, send_sem=ss, recv_sem=rs, device_id=to, device_id_type=MESH
        )

    def req_copy(p):
        return copy(req.at[p], asked_v.at[p], req_ss.at[p], req_rs.at[p], there(p))

    def leaf_copy(p):
        return copy(send.at[p], leaf_out.at[p], leaf_ss.at[p], leaf_rs.at[p], back(p))

    def mu_copy(p):
        return copy(mu_out.at[REACH], mu_out.at[p], mu_ss.at[p], mu_rs.at[p], back(p))

    def z_copy(i):
        return copy(part, zbuf.at[grp], z_ss.at[i], z_rs.at[i], z_peer(i))

    def y_copy(i):
        own = coarse_out.at[box]
        return copy(own, own, y_ss.at[i], y_rs.at[i], y_peer(i))

    def x_copy(i):
        own = coarse_out.at[pl.ds(bx * 8, 8)]
        return copy(own, own, x_ss.at[i], x_rs.at[i], x_peer(i))

    def each(count, first, act):
        def one(i, c):
            act(i + first)
            return c

        lax.fori_loop(0, count, one, 0)

    each(SLOTS - 1, 0, lambda i: req_copy(slot_of(i)).start())
    left = left_half()
    loads[0].wait()
    loads[1].wait()

    def boxes(i, c):
        for q in range(2):
            b = i * 8 + q * 4
            points = [
                charges[:, pl.ds(pl.multiple_of((b + j) * 256, 256), 256)] for j in range(4)
            ]
            o = lax.dot_general(
                jnp.concatenate(points, axis=0),
                basis[pl.ds(b, 4)].reshape(256, 256),
                NT,
                preferred_element_type=F32,
            )
            for h in range(2):
                lanes = slice(h * 128, (h + 1) * 128)
                pair = jnp.where(
                    left, o[h * 32 : h * 32 + 16, lanes], o[h * 32 + 16 : h * 32 + 32, lanes]
                )
                turned = pltpu.roll(pair, 64, 1)
                leaf[b + 2 * h] = jnp.where(left, pair, turned).astype(BF)
                leaf[b + 2 * h + 1] = jnp.where(left, turned, pair).astype(BF)
                place = pl.ds(pl.multiple_of((i * 4 + q * 2 + h) * 16, 16), 16)
                own_leaf[place, :] = pair.astype(BF)
        return c

    lax.fori_loop(0, LEAFS // 8, boxes, 0)


    def turn_part(k):
        first, last, per = TURN_PARTS[k]
        turn(coupling, weights, first, last, per)
        store_part(k).start()

    def store_part(k):
        span = pl.ds(TURN_PARTS[k][0] * 4, (TURN_PARTS[k][1] - TURN_PARTS[k][0]) * 4)
        return pltpu.make_async_copy(weights.at[span], weights_any.at[span], out_s.at[k])

    asked_v[REACH] = jnp.zeros((1, 128), I32)
    each(SLOTS - 1, 0, lambda i: req_copy(slot_of(i)).wait_recv())
    local = pltpu.make_async_copy(asked_v, asked_s, loc_s.at[0])
    local.start()
    local.wait()

    def serve(i):
        p = slot_of(i)
        for q in range(ROOM // 2):
            a = leaf[asked_s[p, 0, 2 * q]]
            b = leaf[asked_s[p, 0, 2 * q + 1]]
            send[p, q * 16 : (q + 1) * 16, :] = jnp.where(left, a, b)
        leaf_copy(p).start()

    each(SLOTS - 1, 0, serve)

    def mids(i, c):
        for k in range(4):
            t = i * 4 + k
            split[t] = lift(
                [leaf[t * 8 + j] for j in range(8)], [transfer[t * 8 + j] for j in range(8)]
            ).astype(BF)
        return c

    lax.fori_loop(0, 4, mids, 0)
    mid[...] = weave([split[t] for t in range(16)]).reshape(16, 16, 128)
    for q in range(8):
        mu_out[REACH, q * 16 : (q + 1) * 16, :] = jnp.where(left, mid[2 * q], mid[2 * q + 1])
    upper = []
    for t in range(2):
        children = range(t * 8, t * 8 + 8)
        sums = lift([mid[j] for j in children], [transfer[128 + j] for j in children])
        upper.append(sums.astype(BF))
    upper = weave(upper)
    upper = [upper[0:16], upper[16:32]]
    mu_out[REACH, 128:144, :] = jnp.where(left, upper[0], upper[1])
    part[...] = jnp.zeros(part.shape, F32)
    part[:, 0:32] = lift(upper, [transfer[144], transfer[145]])
    zbuf[grp] = part[...]
    each(3, 1, lambda i: z_copy(i).start())
    each(SLOTS - 1, 0, lambda i: mu_copy(slot_of(i)).start())
    loads[2].wait()
    turn_part(0)
    each(3, 1, lambda i: z_copy(i).wait())
    whole = (zbuf[0] + zbuf[1] + zbuf[2] + zbuf[3]).astype(BF)
    coarse_out[box] = weave([whole[:, 0:32]])
    each(7, 1, lambda i: y_copy(i).start())
    turn_part(1)
    each(7, 1, lambda i: y_copy(i).wait())
    each(3, 1, lambda i: x_copy(i).start())
    turn_part(2)
    each(3, 1, lambda i: x_copy(i).wait())

    each(SLOTS - 1, 0, lambda i: req_copy(slot_of(i)).wait_send())
    each(SLOTS - 1, 0, lambda i: mu_copy(slot_of(i)).wait())
    each(SLOTS - 1, 0, lambda i: leaf_copy(slot_of(i)).wait())
    for k in range(len(TURN_PARTS)):
        store_part(k).wait()


def exchange(req, charges, basis, transfer, coupling):
    sem = pltpu.SemaphoreType.DMA
    return pl.pallas_call(
        exchange_kernel,
        out_shape=(
            jax.ShapeDtypeStruct((SLOTS, 256, 128), BF),
            jax.ShapeDtypeStruct((SLOTS, 144, 128), BF),
            jax.ShapeDtypeStruct((32, 16, 128), BF),
            jax.ShapeDtypeStruct((1024, 128), BF),
            jax.ShapeDtypeStruct((KINDS, 4, 32, 128), BF),
        ),
        in_specs=[VMEM, ANY, ANY, VMEM, ANY],
        out_specs=[VMEM] * 4 + [ANY],
        scratch_shapes=[
            pltpu.VMEM((SLOTS, 1, 128), I32),
            pltpu.SMEM((SLOTS, 1, 128), I32),
            pltpu.VMEM((SLOTS, 256, 128), BF),
            pltpu.VMEM((4, 32, 128), F32),
            pltpu.VMEM((KINDS, 128, 128), BF),
            pltpu.VMEM((KINDS, 4, 32, 128), BF),
            sem((3,)),
            sem((len(TURN_PARTS),)),
            pltpu.VMEM((16, 32768), BF),
            pltpu.VMEM((LEAFS, 64, 256), BF),
            pltpu.VMEM((LEAFS, 16, 128), BF),
            pltpu.VMEM((16, 32, 32), BF),
            pltpu.VMEM((16, 16, 128), BF),
            pltpu.VMEM((32, 128), F32),
        ]
        + [sem((SLOTS,))] * 7
        + [sem((8,))] * 6,
        compiler_params=pltpu.CompilerParams(
            collective_id=0, has_side_effects=True, vmem_limit_bytes=60 << 20
        ),
        name="exchange",
    )(req, charges, basis, transfer, coupling)


def far_kernel(
    req, meta, own_leaf, leaf_in, mu_in, coarse_in, transfer,
    rows_any, kinds_any, weights_any, basis_any, out,
    rows_idx, kinds_idx, table, weights, basis, local, parents, in_s,
):
    loads = [
        pltpu.make_async_copy(rows_any, rows_idx, in_s.at[0]),
        pltpu.make_async_copy(kinds_any, kinds_idx, in_s.at[1]),
        pltpu.make_async_copy(weights_any, weights, in_s.at[2]),
    ]
    load_basis = pltpu.make_async_copy(basis_any, basis, in_s.at[3])
    for load in loads:
        load.start()
    l = iota((128, 512), 0)
    n = iota((128, 512), 1)
    spread = jnp.where(l == (n >> 7) * 32 + (n & 31), 1.0, 0.0).astype(BF)
    table[ZERO_ROW] = jnp.zeros((32, 128), BF)

    def fill(block, places):
        y = jnp.dot(block, spread, preferred_element_type=F32).astype(BF)
        for i, (a, b, h) in enumerate(places):
            s = slice(i * 16, (i + 1) * 16)
            first = [y[s, 0:128], y[s, 128:256]]
            table[a] = jnp.concatenate([first[h], first[1 - h]], axis=0)
            if b is not None:
                last = [y[s, 256:384], y[s, 384:512]]
                table[b] = jnp.concatenate([last[h], last[1 - h]], axis=0)

    def mu_places(p):
        mid = [(MID_ROW + p * 16 + 2 * i, MID_ROW + p * 16 + 2 * i + 1, 1) for i in range(8)]
        return mid + [(UPPER_ROW + p * 2, UPPER_ROW + p * 2 + 1, 0)]

    def peers(i, c):
        for k in range(3):
            peer(i * 3 + k)
        return c

    def peer(i):
        p = slot_of(i)
        fill(
            leaf_in[p],
            [
                (p * LEAFS + req[p, 0, 2 * q], p * LEAFS + req[p, 0, 2 * q + 1], 0)
                for q in range(16)
            ],
        )
        fill(mu_in[p], mu_places(p))

    lax.fori_loop(0, (SLOTS - 1) // 3, peers, 0)
    fill(mu_in[REACH], mu_places(REACH))

    def own(i, c):
        base = REACH * LEAFS + i * 32
        fill(
            own_leaf[pl.ds(pl.multiple_of(i * 256, 256), 256), :],
            [(base + 2 * q, base + 2 * q + 1, 0) for q in range(16)],
        )
        return c

    lax.fori_loop(0, 4, own, 0)

    def coarse(i, c):
        fill(
            coarse_in[pl.ds(pl.multiple_of(i * 128, 128), 128), :],
            [(COARSE_ROW + i * 8 + q, None, 1) for q in range(8)],
        )
        return c

    lax.fori_loop(0, 4, coarse, 0)

    for load in loads:
        load.wait()
    load_basis.start()
    lane = iota((32, 128), 1)
    m1, m2, m3 = lane < 32, lane < 64, lane < 96
    left = iota((16, 128), 1) < 64

    def merge(a, b, c, d):
        return jnp.where(m2, jnp.where(m1, a, b), jnp.where(m3, c, d))

    def one(t, batches):
        acc = None
        for b in range(batches):
            cols, quads = [], []
            for g in range(2):
                base = b * 16 + g * 8
                cols.append(
                    jnp.concatenate([weights[kinds_idx[t * 256 + base + j]] for j in range(8)], axis=0)
                )
                quads.append(
                    jnp.concatenate(
                        [
                            merge(*[table[rows_idx[t * 256 + base + q * 4 + i]] for i in range(4)])
                            for q in range(2)
                        ],
                        axis=1,
                    )
                )
            d = jnp.dot(
                jnp.concatenate(quads, axis=0),
                jnp.concatenate(cols, axis=1),
                preferred_element_type=F32,
            )
            acc = d if acc is None else acc + d
        u = jnp.where(
            left, acc[0:16, 0:128] + acc[32:48, 128:256], acc[16:32, 0:128] + acc[48:64, 128:256]
        )
        local[t] = u + pltpu.roll(u, 64, 1)

    def four(i, c, batches):
        for k in range(4):
            one(meta[0, i * 4 + k], batches)
        return c

    first = 0
    for batches in range(SLOT_PAD // 16, 5, -1):
        last = meta[1, batches - 1] if batches > 6 else TARGETS // 4
        lax.fori_loop(first, last, functools.partial(four, batches=batches), 0)
        first = last

    load_basis.wait()
    (coarse_field,) = unweave([local[146].astype(BF)])
    upper_fields = unweave(
        lowered(coarse_field, [transfer[144], transfer[145]], [local[144], local[145]])
    )
    mid_fields = []
    for u in range(2):
        children = range(u * 8, u * 8 + 8)
        mid_fields += lowered(
            upper_fields[u], [transfer[128 + m] for m in children], [local[128 + m] for m in children]
        )
    for m, field in enumerate(unweave(mid_fields)):
        parents[m] = field

    zero = jnp.zeros((16, 128), BF)

    def boxes(m):
        fields = lowered(
            parents[m],
            [transfer[m * 8 + j] for j in range(8)],
            [local[m * 8 + j] for j in range(8)],
        )
        for q in range(2):
            rows = []
            for j in range(4):
                f = fields[q * 4 + j]
                f = jnp.where(left, zero, f) if j % 2 else jnp.where(left, f, zero)
                rows.append(jnp.concatenate([zero, f] if j > 1 else [f, zero], axis=1))
            b = m * 8 + q * 4
            points = jnp.dot(
                jnp.concatenate(rows, axis=0),
                basis[pl.ds(b, 4)].reshape(256, 256),
                preferred_element_type=F32,
            ).astype(BF)
            for j in range(4):
                place = pl.ds(pl.multiple_of((b + j) * 256, 256), 256)
                out[:, place] = points[j * 16 : (j + 1) * 16]

    def two(i, c):
        boxes(2 * i)
        boxes(2 * i + 1)
        return c

    lax.fori_loop(0, 8, two, 0)


def far(rows_idx, kinds_idx, req, meta, own_leaf, leaf_in, mu_in, coarse_in, transfer, weights, basis):
    return pl.pallas_call(
        far_kernel,
        out_shape=jax.ShapeDtypeStruct((16, LEAFS * 256), BF),
        in_specs=[SMEM] * 2 + [VMEM] * 5 + [ANY] * 4,
        out_specs=VMEM,
        scratch_shapes=[
            pltpu.SMEM((TARGETS * 256,), I32),
            pltpu.SMEM((TARGETS * 256,), I32),
            pltpu.VMEM((TABLE_ROWS, 32, 128), BF),
            pltpu.VMEM((4 * KINDS, 32, 128), BF),
            pltpu.VMEM((LEAFS, 64, 256), BF),
            pltpu.VMEM((TARGETS, 16, 128), F32),
            pltpu.VMEM((16, 32, 32), BF),
            pltpu.SemaphoreType.DMA((4,)),
        ],
        compiler_params=pltpu.CompilerParams(vmem_limit_bytes=60 << 20),
        name="far",
    )(
        req, meta, own_leaf, leaf_in, mu_in, coarse_in, transfer, rows_idx, kinds_idx, weights, basis
    )


def on_device(
    charges, leaf_basis, transfer0, transfer1, transfer2, coupling,
    lists0, lists1, lists2, lists3, kinds0, kinds1, kinds2, kinds3,
):
    transfer = jnp.concatenate([transfer0, transfer1, transfer2], axis=0).reshape(146, 32, 128)
    by_kind = coupling.reshape(4, KINDS, 32, 128).transpose(1, 2, 0, 3).reshape(KINDS, 128, 128)
    rows_idx, kinds_idx, req, meta = plan(
        (lists0, lists1, lists2, lists3), (kinds0, kinds1, kinds2, kinds3)
    )
    leaf_in, mu_in, coarse_in, own_leaf, weights = exchange(
        req, charges, leaf_basis, transfer, by_kind
    )
    return far(
        rows_idx.reshape(-1), kinds_idx.reshape(-1), req, meta, own_leaf, leaf_in, mu_in,
        coarse_in.reshape(512, 128), transfer, weights.reshape(4 * KINDS, 32, 128), leaf_basis,
    )


def solution(mesh):
    both = ("boxes", "grp")
    in_specs = (
        P(None, both),
        P(both, None, None),
        P(both, None),
        P(both, None),
        P(both, None),
        P(),
        P(both, None),
        P(both, None),
        P(both, None),
        P("boxes", None),
        P(both, None),
        P(both, None),
        P(both, None),
        P("boxes", None),
    )
    return jax.shard_map(
        on_device, mesh=mesh, in_specs=in_specs, out_specs=P(None, both), check_vma=False
    )
```

```python
import functools

import jax
import jax.numpy as jnp
from jax import lax
from jax.experimental import pallas as pl
from jax.experimental.pallas import tpu as pltpu
from jax.sharding import PartitionSpec as P

BF = jnp.bfloat16
F32 = jnp.float32
I32 = jnp.int32
MESH = pl.DeviceIdType.MESH

DEV = 128
REACH = 13
SLOTS = 28
LEAFS = 128
ROOM = 32
SLOT_PAD = 192
TARGETS = 148
ZERO_ROW = SLOTS * LEAFS
MID_ROW = ZERO_ROW + 8
UPPER_ROW = MID_ROW + SLOTS * 16
COARSE_ROW = UPPER_ROW + SLOTS * 2
TABLE_ROWS = COARSE_ROW + 32
KINDS = 316
VMEM = pl.BlockSpec(memory_space=pltpu.VMEM)
ANY = pl.BlockSpec(memory_space=pl.ANY)
SMEM = pl.BlockSpec(memory_space=pltpu.SMEM)
TURN_PARTS = ((0, 10, 2), (10, 43, 3), (43, 79, 3))
NT = (((1,), (1,)), ((), ()))


def iota(shape, dim):
    return lax.broadcasted_iota(I32, shape, dim)


def plan_kernel(
    l0_across, k0_across, l1_any, l2_any, l3_any, k1_any, k2_any, k3_any,
    rows_flat, kinds_flat, req_out, meta,
    rows_out, kinds_out, l0, k0, pad, l1, l2, l3, k1, k2, k3, in_s,
):
    loads = [
        pltpu.make_async_copy(src, dst, in_s.at[i])
        for i, (src, dst) in enumerate(
            ((l1_any, l1), (l2_any, l2), (l3_any, l3), (k1_any, k1), (k2_any, k2), (k3_any, k3))
        )
    ]
    for load in loads:
        load.start()
    pad[...] = jnp.zeros(pad.shape, I32)
    for across, tiled in ((l0_across, l0), (k0_across, k0)):
        pad[0:189, :] = across[...]
        tiled[...] = pad[...].T
    for load in loads:
        load.wait()
    me = lax.axis_index("boxes") * 4 + lax.axis_index("grp")
    rows_out[...] = jnp.full(rows_out.shape, ZERO_ROW, I32)
    kinds_out[...] = jnp.zeros(kinds_out.shape, I32)
    start = 0
    for level, (lists, kinds, count, offset) in enumerate(
        ((l0, k0, 128, 0), (l1, k1, 16, MID_ROW), (l2, k2, 2, UPPER_ROW))
    ):
        ids = lists[...][:, 0:189]
        whole = DEV * count
        rel = lax.rem(ids - (me - REACH) * count + whole, whole)
        far = (REACH + DEV // 2) * count
        rel = jnp.where(rel >= far, rel - far + (SLOTS - 1) * count, rel)
        rows_out[start : start + count, 0:189] = jnp.where(ids >= 0, rel + offset, ZERO_ROW)
        kinds_out[start : start + count, 0:189] = kinds[...][:, 0:189] * 4 + level
        start += count
    ids = l3[...]
    rows_out[start : start + 1, 0:189] = jnp.where(ids >= 0, ids + COARSE_ROW, ZERO_ROW)
    kinds_out[start : start + 1, 0:189] = k3[...] * 4 + 3
    for flat, tiled in ((rows_flat, rows_out), (kinds_flat, kinds_out)):
        flat[pl.ds(0, TARGETS, stride=2), :] = tiled[:, 0:128]
        flat[pl.ds(1, TARGETS, stride=2), 0 : SLOT_PAD - 128] = tiled[:, 128:SLOT_PAD]

    live = jnp.where(rows_out[...] != ZERO_ROW, 1.0, 0.0).astype(BF)
    down = jnp.dot(live, jnp.ones((SLOT_PAD, 256), BF), preferred_element_type=F32)[:, :TARGETS]
    across = lax.dot_general(jnp.ones((8, SLOT_PAD), BF), live, NT, preferred_element_type=F32)
    down = (down.astype(I32) + 15) >> 4
    across = (across[0:1].astype(I32) + 15) >> 4
    t_down, t_across = iota((TARGETS, TARGETS), 0), iota((TARGETS, TARGETS), 1)
    before = (across > down) | ((across == down) & (t_across < t_down))
    place = jnp.sum(jnp.where(before, 1.0, 0.0), axis=1, keepdims=True)
    here = place == t_across.astype(F32)
    order = jnp.sum(jnp.where(here, t_down.astype(F32), 0.0), axis=0, keepdims=True).astype(I32)
    meta[...] = jnp.zeros(meta.shape, I32)
    meta[0:1, 0:TARGETS] = order
    sub = iota((16, TARGETS), 0)
    over = jnp.sum(jnp.where(across > sub, 1.0, 0.0), axis=1, keepdims=True).astype(I32)
    ends = jnp.where(iota((16, 256), 1) == iota((16, 256), 0), (over + 3) >> 2, 0)
    meta[1:2, :] = jnp.sum(ends, axis=0, keepdims=True)

    sub_lo = iota((LEAFS, SLOT_PAD), 0)
    sub_hi = iota((32, SLOT_PAD), 0)

    def mark(i, seen):
        lo, hi = [], []
        for k in range(2):
            row = rows_out[pl.ds(2 * i + k, 1), :]
            lo.append(jnp.where(sub_lo == (row & 127), 1.0, 0.0).astype(BF))
            hi.append(jnp.where(sub_hi == (row >> 7), 1.0, 0.0).astype(BF))
        return seen + lax.dot_general(
            jnp.concatenate(hi, axis=0), jnp.concatenate(lo, axis=0), NT, preferred_element_type=F32
        )

    seen = lax.fori_loop(0, LEAFS // 2, mark, jnp.zeros((64, 2 * LEAFS), F32), unroll=4)
    seen = seen[0:32, 0:LEAFS] + seen[32:64, LEAFS:]
    needed = seen > 0.5
    lane = iota((32, LEAFS), 1)
    upto = (
        iota((LEAFS, LEAFS), 0) <= iota((LEAFS, LEAFS), 1)
    )
    rank = jnp.dot(
        jnp.where(needed, 1.0, 0.0).astype(BF),
        jnp.where(upto, 1.0, 0.0).astype(BF),
        preferred_element_type=F32,
    )
    rank = jnp.where(needed, rank, 0.0)
    lane_f = lane.astype(F32)
    asked = jnp.zeros((32, LEAFS), F32)
    for q in range(ROOM):
        pick = jnp.sum(jnp.where(rank == q + 1.0, lane_f, 0.0), axis=1, keepdims=True)
        asked = jnp.where(lane == q, pick, asked)
    asked = asked.astype(I32)
    for h in range(SLOTS):
        req_out[h] = asked[h : h + 1, :]


def plan(lists, kinds):
    return pl.pallas_call(
        plan_kernel,
        out_shape=(
            jax.ShapeDtypeStruct((2 * TARGETS, 128), I32),
            jax.ShapeDtypeStruct((2 * TARGETS, 128), I32),
            jax.ShapeDtypeStruct((SLOTS, 1, 128), I32),
            jax.ShapeDtypeStruct((8, 256), I32),
        ),
        in_specs=[VMEM] * 2 + [ANY] * 6,
        out_specs=[VMEM] * 4,
        scratch_shapes=[pltpu.VMEM((TARGETS, SLOT_PAD), I32)] * 2
        + [pltpu.VMEM((LEAFS, 256), I32)] * 2
        + [pltpu.VMEM((256, LEAFS), I32)]
        + [pltpu.VMEM((n, 189), I32) for n in (16, 2, 1)] * 2
        + [pltpu.SemaphoreType.DMA((6,))],
        compiler_params=pltpu.CompilerParams(vmem_limit_bytes=60 << 20),
        name="plan",
    )(lists[0].T, kinds[0].T, *lists[1:], *kinds[1:])


def left_half():
    return iota((16, 128), 1) < 64


def lift(children, matrices):
    left = left_half()
    zero = jnp.zeros((16, 128), BF)
    rows = [
        jnp.concatenate([jnp.where(left, m, zero), jnp.where(left, zero, m)], axis=0)
        for m in children
    ]
    return lax.dot_general(
        jnp.concatenate(rows, axis=1),
        jnp.concatenate(matrices, axis=1),
        NT,
        preferred_element_type=F32,
    )


def weave(splits):
    lane = iota((32, 128), 1) & 63
    total = None
    for h in range(2):
        put = jnp.where(lane == 2 * iota((32, 128), 0) + h, 1.0, 0.0).astype(BF)
        rows = jnp.concatenate([x[h * 16 : (h + 1) * 16] for x in splits], axis=0)
        part = jnp.dot(rows, put, preferred_element_type=F32)
        total = part if total is None else total + part
    return total.astype(BF)


def unweave(blocks):
    x = jnp.concatenate(blocks, axis=0)
    parts = []
    for h in range(2):
        put = jnp.where(iota((128, 32), 0) == 2 * iota((128, 32), 1) + h, 1.0, 0.0).astype(BF)
        parts.append(jnp.dot(x, put, preferred_element_type=F32))
    return [
        jnp.concatenate([p[i * 16 : (i + 1) * 16] for p in parts], axis=0).astype(BF)
        for i in range(len(blocks))
    ]


def lowered(parent, matrices, locals_):
    left = left_half()
    o = jnp.dot(parent, jnp.concatenate(matrices, axis=1), preferred_element_type=F32)
    fields = []
    for i, local in enumerate(locals_):
        e = o[:, i * 128 : (i + 1) * 128]
        u = jnp.where(left, e[0:16], e[16:32])
        fields.append((local + (u + pltpu.roll(u, 64, 1))).astype(BF))
    return fields


def turn(coupling, weights, first, last, per):
    eye = jnp.where(iota((128, 128), 0) == iota((128, 128), 1), 1.0, 0.0).astype(BF)
    row, col = iota((256, 256), 0), iota((256, 256), 1)
    fits = (col & 63) == 2 * ((row & 127) >> 2) + (row >> 7)
    pick = [
        jnp.where(fits & (((col >> 6) ^ h) == (row & 3)), 1.0, 0.0).astype(BF) for h in range(2)
    ]
    left = iota((32, 128), 1) < 64

    def step(i, c):
        base = (first + i * per) * 4
        rows = [[], []]
        for j in range(2 * per):
            pair = coupling[pl.ds(base + 2 * j, 2)].reshape(256, 128)
            t = lax.dot_general(eye, pair, NT, preferred_element_type=F32).astype(BF)
            for k in range(2):
                y = t[:, k * 128 : (k + 1) * 128]
                for h in range(2):
                    a = y[h * 32 : h * 32 + 32]
                    b = y[64 + h * 32 : 64 + h * 32 + 32]
                    rows[h].append(jnp.concatenate([a, b], axis=1))
        half = [
            jnp.dot(jnp.concatenate(rows[h], axis=0), pick[h], preferred_element_type=F32).astype(BF)
            for h in range(2)
        ]
        for k in range(4 * per):
            for p in range(2):
                a = half[0][k * 32 : k * 32 + 32, p * 128 : (p + 1) * 128]
                b = half[1][k * 32 : k * 32 + 32, p * 128 : (p + 1) * 128]
                weights[base + k, 2 * p] = jnp.where(left, a, b)
                weights[base + k, 2 * p + 1] = jnp.where(left, b, a)
        return c

    lax.fori_loop(0, (last - first) // per, step, 0)


def slot_of(i):
    return i + (i + 15) // 28


def offset_of(p):
    return p - REACH + (DEV // 2 - SLOTS + 1 + REACH) * (p // (SLOTS - 1))


def exchange_kernel(
    req, charges_any, basis_any, transfer, coupling_any,
    leaf_out, mu_out, coarse_out, own_leaf, weights_any,
    asked_v, asked_s, send, zbuf, coupling, weights, in_s, out_s,
    charges, basis, leaf, split, mid, part,
    req_ss, req_rs, loc_s, leaf_ss, leaf_rs, mu_ss, mu_rs, z_ss, z_rs, y_ss, y_rs, x_ss, x_rs,
):
    box = lax.axis_index("boxes")
    grp = lax.axis_index("grp")
    me = box * 4 + grp
    bx = box // 8
    by = box % 8

    def there(p):
        t = (me + offset_of(p) + DEV) % DEV
        return (t // 4, t % 4)

    def back(p):
        t = (me - offset_of(p) + DEV) % DEV
        return (t // 4, t % 4)

    def z_peer(i):
        return (box, (grp + i) % 4)

    def y_peer(i):
        return (bx * 8 + (by + i) % 8, grp)

    def x_peer(i):
        return (((bx + i) % 4) * 8 + by, grp)

    loads = [
        pltpu.make_async_copy(charges_any, charges, in_s.at[0]),
        pltpu.make_async_copy(basis_any, basis, in_s.at[1]),
        pltpu.make_async_copy(coupling_any, coupling, in_s.at[2]),
    ]
    for load in loads:
        load.start()
    barrier = pltpu.get_barrier_semaphore()

    def greet(to, first, count):
        def one(i, c):
            pl.semaphore_signal(barrier, inc=1, device_id=to(i + first), device_id_type=MESH)
            return c

        lax.fori_loop(0, count, one, 0)

    greet(lambda i: there(slot_of(i)), 0, SLOTS - 1)
    greet(z_peer, 1, 3)
    greet(y_peer, 1, 7)
    greet(x_peer, 1, 3)
    pl.semaphore_wait(barrier, SLOTS - 1 + 13)

    def copy(src, dst, ss, rs, to):
        return pltpu.make_async_remote_copy(
            src_ref=src, dst_ref=dst, send_sem=ss, recv_sem=rs, device_id=to, device_id_type=MESH
        )

    def req_copy(p):
        return copy(req.at[p], asked_v.at[p], req_ss.at[p], req_rs.at[p], there(p))

    def leaf_copy(p):
        return copy(send.at[p], leaf_out.at[p], leaf_ss.at[p], leaf_rs.at[p], back(p))

    def mu_copy(p):
        return copy(mu_out.at[REACH], mu_out.at[p], mu_ss.at[p], mu_rs.at[p], back(p))

    def z_copy(i):
        return copy(part, zbuf.at[grp], z_ss.at[i], z_rs.at[i], z_peer(i))

    def y_copy(i):
        own = coarse_out.at[box]
        return copy(own, own, y_ss.at[i], y_rs.at[i], y_peer(i))

    def x_copy(i):
        own = coarse_out.at[pl.ds(bx * 8, 8)]
        return copy(own, own, x_ss.at[i], x_rs.at[i], x_peer(i))

    def each(count, first, act):
        def one(i, c):
            act(i + first)
            return c

        lax.fori_loop(0, count, one, 0)

    each(SLOTS - 1, 0, lambda i: req_copy(slot_of(i)).start())
    left = left_half()
    loads[0].wait()
    loads[1].wait()

    def boxes(i, c):
        for q in range(2):
            b = i * 8 + q * 4
            points = [
                charges[:, pl.ds(pl.multiple_of((b + j) * 256, 256), 256)] for j in range(4)
            ]
            o = lax.dot_general(
                jnp.concatenate(points, axis=0),
                basis[pl.ds(b, 4)].reshape(256, 256),
                NT,
                preferred_element_type=F32,
            )
            for h in range(2):
                lanes = slice(h * 128, (h + 1) * 128)
                pair = jnp.where(
                    left, o[h * 32 : h * 32 + 16, lanes], o[h * 32 + 16 : h * 32 + 32, lanes]
                )
                turned = pltpu.roll(pair, 64, 1)
                leaf[b + 2 * h] = jnp.where(left, pair, turned).astype(BF)
                leaf[b + 2 * h + 1] = jnp.where(left, turned, pair).astype(BF)
                place = pl.ds(pl.multiple_of((i * 4 + q * 2 + h) * 16, 16), 16)
                own_leaf[place, :] = pair.astype(BF)
        return c

    lax.fori_loop(0, LEAFS // 8, boxes, 0)


    def turn_part(k):
        first, last, per = TURN_PARTS[k]
        turn(coupling, weights, first, last, per)
        store_part(k).start()

    def store_part(k):
        span = pl.ds(TURN_PARTS[k][0] * 4, (TURN_PARTS[k][1] - TURN_PARTS[k][0]) * 4)
        return pltpu.make_async_copy(weights.at[span], weights_any.at[span], out_s.at[k])

    def mids(i, c):
        for k in range(4):
            t = i * 4 + k
            split[t] = lift(
                [leaf[t * 8 + j] for j in range(8)], [transfer[t * 8 + j] for j in range(8)]
            ).astype(BF)
        return c

    lax.fori_loop(0, 4, mids, 0)
    mid[...] = weave([split[t] for t in range(16)]).reshape(16, 16, 128)
    for q in range(8):
        mu_out[REACH, q * 16 : (q + 1) * 16, :] = jnp.where(left, mid[2 * q], mid[2 * q + 1])
    upper = []
    for t in range(2):
        children = range(t * 8, t * 8 + 8)
        sums = lift([mid[j] for j in children], [transfer[128 + j] for j in children])
        upper.append(sums.astype(BF))
    upper = weave(upper)
    upper = [upper[0:16], upper[16:32]]
    mu_out[REACH, 128:144, :] = jnp.where(left, upper[0], upper[1])
    part[...] = jnp.zeros(part.shape, F32)
    part[:, 0:32] = lift(upper, [transfer[144], transfer[145]])
    zbuf[grp] = part[...]
    each(3, 1, lambda i: z_copy(i).start())
    each(SLOTS - 1, 0, lambda i: mu_copy(slot_of(i)).start())
    asked_v[REACH] = jnp.zeros((1, 128), I32)
    each(SLOTS - 1, 0, lambda i: req_copy(slot_of(i)).wait_recv())
    local = pltpu.make_async_copy(asked_v, asked_s, loc_s.at[0])
    local.start()
    local.wait()

    def serve(i):
        p = slot_of(i)
        for q in range(ROOM // 2):
            a = leaf[asked_s[p, 0, 2 * q]]
            b = leaf[asked_s[p, 0, 2 * q + 1]]
            send[p, q * 16 : (q + 1) * 16, :] = jnp.where(left, a, b)
        leaf_copy(p).start()

    each(SLOTS - 1, 0, serve)

    loads[2].wait()
    turn_part(0)
    each(3, 1, lambda i: z_copy(i).wait())
    whole = (zbuf[0] + zbuf[1] + zbuf[2] + zbuf[3]).astype(BF)
    coarse_out[box] = weave([whole[:, 0:32]])
    each(7, 1, lambda i: y_copy(i).start())
    turn_part(1)
    each(7, 1, lambda i: y_copy(i).wait())
    each(3, 1, lambda i: x_copy(i).start())
    turn_part(2)
    each(3, 1, lambda i: x_copy(i).wait())

    each(SLOTS - 1, 0, lambda i: req_copy(slot_of(i)).wait_send())
    each(SLOTS - 1, 0, lambda i: mu_copy(slot_of(i)).wait())
    each(SLOTS - 1, 0, lambda i: leaf_copy(slot_of(i)).wait())
    for k in range(len(TURN_PARTS)):
        store_part(k).wait()


def exchange(req, charges, basis, transfer, coupling):
    sem = pltpu.SemaphoreType.DMA
    return pl.pallas_call(
        exchange_kernel,
        out_shape=(
            jax.ShapeDtypeStruct((SLOTS, 256, 128), BF),
            jax.ShapeDtypeStruct((SLOTS, 144, 128), BF),
            jax.ShapeDtypeStruct((32, 16, 128), BF),
            jax.ShapeDtypeStruct((1024, 128), BF),
            jax.ShapeDtypeStruct((KINDS, 4, 32, 128), BF),
        ),
        in_specs=[VMEM, ANY, ANY, VMEM, ANY],
        out_specs=[VMEM] * 4 + [ANY],
        scratch_shapes=[
            pltpu.VMEM((SLOTS, 1, 128), I32),
            pltpu.SMEM((SLOTS, 1, 128), I32),
            pltpu.VMEM((SLOTS, 256, 128), BF),
            pltpu.VMEM((4, 32, 128), F32),
            pltpu.VMEM((KINDS, 128, 128), BF),
            pltpu.VMEM((KINDS, 4, 32, 128), BF),
            sem((3,)),
            sem((len(TURN_PARTS),)),
            pltpu.VMEM((16, 32768), BF),
            pltpu.VMEM((LEAFS, 64, 256), BF),
            pltpu.VMEM((LEAFS, 16, 128), BF),
            pltpu.VMEM((16, 32, 32), BF),
            pltpu.VMEM((16, 16, 128), BF),
            pltpu.VMEM((32, 128), F32),
        ]
        + [sem((SLOTS,))] * 7
        + [sem((8,))] * 6,
        compiler_params=pltpu.CompilerParams(
            collective_id=0, has_side_effects=True, vmem_limit_bytes=60 << 20
        ),
        name="exchange",
    )(req, charges, basis, transfer, coupling)


def far_kernel(
    req, meta, own_leaf, leaf_in, mu_in, coarse_in, transfer,
    rows_any, kinds_any, weights_any, basis_any, out,
    rows_idx, kinds_idx, table, weights, basis, local, parents, in_s,
):
    loads = [
        pltpu.make_async_copy(rows_any, rows_idx, in_s.at[0]),
        pltpu.make_async_copy(kinds_any, kinds_idx, in_s.at[1]),
        pltpu.make_async_copy(weights_any, weights, in_s.at[2]),
    ]
    load_basis = pltpu.make_async_copy(basis_any, basis, in_s.at[3])
    for load in loads:
        load.start()
    l = iota((128, 512), 0)
    n = iota((128, 512), 1)
    spread = jnp.where(l == (n >> 7) * 32 + (n & 31), 1.0, 0.0).astype(BF)
    table[ZERO_ROW] = jnp.zeros((32, 128), BF)

    def fill(block, places):
        y = jnp.dot(block, spread, preferred_element_type=F32).astype(BF)
        for i, (a, b, h) in enumerate(places):
            s = slice(i * 16, (i + 1) * 16)
            first = [y[s, 0:128], y[s, 128:256]]
            table[a] = jnp.concatenate([first[h], first[1 - h]], axis=0)
            if b is not None:
                last = [y[s, 256:384], y[s, 384:512]]
                table[b] = jnp.concatenate([last[h], last[1 - h]], axis=0)

    def mu_places(p):
        mid = [(MID_ROW + p * 16 + 2 * i, MID_ROW + p * 16 + 2 * i + 1, 1) for i in range(8)]
        return mid + [(UPPER_ROW + p * 2, UPPER_ROW + p * 2 + 1, 0)]

    def peers(i, c):
        for k in range(3):
            peer(i * 3 + k)
        return c

    def peer(i):
        p = slot_of(i)
        fill(
            leaf_in[p],
            [
                (p * LEAFS + req[p, 0, 2 * q], p * LEAFS + req[p, 0, 2 * q + 1], 0)
                for q in range(16)
            ],
        )
        fill(mu_in[p], mu_places(p))

    lax.fori_loop(0, (SLOTS - 1) // 3, peers, 0)
    fill(mu_in[REACH], mu_places(REACH))

    def own(i, c):
        base = REACH * LEAFS + i * 32
        fill(
            own_leaf[pl.ds(pl.multiple_of(i * 256, 256), 256), :],
            [(base + 2 * q, base + 2 * q + 1, 0) for q in range(16)],
        )
        return c

    lax.fori_loop(0, 4, own, 0)

    def coarse(i, c):
        fill(
            coarse_in[pl.ds(pl.multiple_of(i * 128, 128), 128), :],
            [(COARSE_ROW + i * 8 + q, None, 1) for q in range(8)],
        )
        return c

    lax.fori_loop(0, 4, coarse, 0)

    for load in loads:
        load.wait()
    load_basis.start()
    lane = iota((32, 128), 1)
    m1, m2, m3 = lane < 32, lane < 64, lane < 96
    left = iota((16, 128), 1) < 64

    def merge(a, b, c, d):
        return jnp.where(m2, jnp.where(m1, a, b), jnp.where(m3, c, d))

    def one(t, batches):
        acc = None
        for b in range(batches):
            cols, quads = [], []
            for g in range(2):
                base = b * 16 + g * 8
                cols.append(
                    jnp.concatenate([weights[kinds_idx[t * 256 + base + j]] for j in range(8)], axis=0)
                )
                quads.append(
                    jnp.concatenate(
                        [
                            merge(*[table[rows_idx[t * 256 + base + q * 4 + i]] for i in range(4)])
                            for q in range(2)
                        ],
                        axis=1,
                    )
                )
            d = jnp.dot(
                jnp.concatenate(quads, axis=0),
                jnp.concatenate(cols, axis=1),
                preferred_element_type=F32,
            )
            acc = d if acc is None else acc + d
        u = jnp.where(
            left, acc[0:16, 0:128] + acc[32:48, 128:256], acc[16:32, 0:128] + acc[48:64, 128:256]
        )
        local[t] = u + pltpu.roll(u, 64, 1)

    def four(i, c, batches):
        for k in range(4):
            one(meta[0, i * 4 + k], batches)
        return c

    first = 0
    for batches in range(SLOT_PAD // 16, 5, -1):
        last = meta[1, batches - 1] if batches > 6 else TARGETS // 4
        lax.fori_loop(first, last, functools.partial(four, batches=batches), 0)
        first = last

    load_basis.wait()
    (coarse_field,) = unweave([local[146].astype(BF)])
    upper_fields = unweave(
        lowered(coarse_field, [transfer[144], transfer[145]], [local[144], local[145]])
    )
    mid_fields = []
    for u in range(2):
        children = range(u * 8, u * 8 + 8)
        mid_fields += lowered(
            upper_fields[u], [transfer[128 + m] for m in children], [local[128 + m] for m in children]
        )
    for m, field in enumerate(unweave(mid_fields)):
        parents[m] = field

    zero = jnp.zeros((16, 128), BF)

    def boxes(m):
        fields = lowered(
            parents[m],
            [transfer[m * 8 + j] for j in range(8)],
            [local[m * 8 + j] for j in range(8)],
        )
        for q in range(2):
            rows = []
            for j in range(4):
                f = fields[q * 4 + j]
                f = jnp.where(left, zero, f) if j % 2 else jnp.where(left, f, zero)
                rows.append(jnp.concatenate([zero, f] if j > 1 else [f, zero], axis=1))
            b = m * 8 + q * 4
            points = jnp.dot(
                jnp.concatenate(rows, axis=0),
                basis[pl.ds(b, 4)].reshape(256, 256),
                preferred_element_type=F32,
            ).astype(BF)
            for j in range(4):
                place = pl.ds(pl.multiple_of((b + j) * 256, 256), 256)
                out[:, place] = points[j * 16 : (j + 1) * 16]

    def two(i, c):
        boxes(2 * i)
        boxes(2 * i + 1)
        return c

    lax.fori_loop(0, 8, two, 0)


def far(rows_idx, kinds_idx, req, meta, own_leaf, leaf_in, mu_in, coarse_in, transfer, weights, basis):
    return pl.pallas_call(
        far_kernel,
        out_shape=jax.ShapeDtypeStruct((16, LEAFS * 256), BF),
        in_specs=[SMEM] * 2 + [VMEM] * 5 + [ANY] * 4,
        out_specs=VMEM,
        scratch_shapes=[
            pltpu.SMEM((TARGETS * 256,), I32),
            pltpu.SMEM((TARGETS * 256,), I32),
            pltpu.VMEM((TABLE_ROWS, 32, 128), BF),
            pltpu.VMEM((4 * KINDS, 32, 128), BF),
            pltpu.VMEM((LEAFS, 64, 256), BF),
            pltpu.VMEM((TARGETS, 16, 128), F32),
            pltpu.VMEM((16, 32, 32), BF),
            pltpu.SemaphoreType.DMA((4,)),
        ],
        compiler_params=pltpu.CompilerParams(vmem_limit_bytes=60 << 20),
        name="far",
    )(
        req, meta, own_leaf, leaf_in, mu_in, coarse_in, transfer, rows_idx, kinds_idx, weights, basis
    )


def on_device(
    charges, leaf_basis, transfer0, transfer1, transfer2, coupling,
    lists0, lists1, lists2, lists3, kinds0, kinds1, kinds2, kinds3,
):
    transfer = jnp.concatenate([transfer0, transfer1, transfer2], axis=0).reshape(146, 32, 128)
    by_kind = coupling.reshape(4, KINDS, 32, 128).transpose(1, 2, 0, 3).reshape(KINDS, 128, 128)
    rows_idx, kinds_idx, req, meta = plan(
        (lists0, lists1, lists2, lists3), (kinds0, kinds1, kinds2, kinds3)
    )
    leaf_in, mu_in, coarse_in, own_leaf, weights = exchange(
        req, charges, leaf_basis, transfer, by_kind
    )
    return far(
        rows_idx.reshape(-1), kinds_idx.reshape(-1), req, meta, own_leaf, leaf_in, mu_in,
        coarse_in.reshape(512, 128), transfer, weights.reshape(4 * KINDS, 32, 128), leaf_basis,
    )


def solution(mesh):
    both = ("boxes", "grp")
    in_specs = (
        P(None, both),
        P(both, None, None),
        P(both, None),
        P(both, None),
        P(both, None),
        P(),
        P(both, None),
        P(both, None),
        P(both, None),
        P("boxes", None),
        P(both, None),
        P(both, None),
        P(both, None),
        P("boxes", None),
    )
    return jax.shard_map(
        on_device, mesh=mesh, in_specs=in_specs, out_specs=P(None, both), check_vma=False
    )
```

```python
import functools

import jax
import jax.numpy as jnp
from jax import lax
from jax.experimental import pallas as pl
from jax.experimental.pallas import tpu as pltpu
from jax.sharding import PartitionSpec as P

BF = jnp.bfloat16
F32 = jnp.float32
I32 = jnp.int32
MESH = pl.DeviceIdType.MESH

DEV = 128
REACH = 13
SLOTS = 28
LEAFS = 128
ROOM = 32
SLOT_PAD = 192
TARGETS = 148
ZERO_ROW = SLOTS * LEAFS
MID_ROW = ZERO_ROW + 8
UPPER_ROW = MID_ROW + SLOTS * 16
COARSE_ROW = UPPER_ROW + SLOTS * 2
TABLE_ROWS = COARSE_ROW + 32
KINDS = 316
VMEM = pl.BlockSpec(memory_space=pltpu.VMEM)
ANY = pl.BlockSpec(memory_space=pl.ANY)
SMEM = pl.BlockSpec(memory_space=pltpu.SMEM)
TURN_PARTS = ((0, 10, 2), (10, 43, 3), (43, 79, 3))
NT = (((1,), (1,)), ((), ()))


def iota(shape, dim):
    return lax.broadcasted_iota(I32, shape, dim)


def plan_kernel(
    l0_across, k0_across, l1_any, l2_any, l3_any, k1_any, k2_any, k3_any,
    rows_flat, kinds_flat, req_out, meta,
    rows_out, kinds_out, l0, k0, pad, l1, l2, l3, k1, k2, k3, in_s,
):
    loads = [
        pltpu.make_async_copy(src, dst, in_s.at[i])
        for i, (src, dst) in enumerate(
            ((l1_any, l1), (l2_any, l2), (l3_any, l3), (k1_any, k1), (k2_any, k2), (k3_any, k3))
        )
    ]
    for load in loads:
        load.start()
    pad[...] = jnp.zeros(pad.shape, I32)
    for across, tiled in ((l0_across, l0), (k0_across, k0)):
        pad[0:189, :] = across[...]
        tiled[...] = pad[...].T
    for load in loads:
        load.wait()
    me = lax.axis_index("boxes") * 4 + lax.axis_index("grp")
    rows_out[...] = jnp.full(rows_out.shape, ZERO_ROW, I32)
    kinds_out[...] = jnp.zeros(kinds_out.shape, I32)
    start = 0
    for level, (lists, kinds, count, offset) in enumerate(
        ((l0, k0, 128, 0), (l1, k1, 16, MID_ROW), (l2, k2, 2, UPPER_ROW))
    ):
        ids = lists[...][:, 0:189]
        whole = DEV * count
        rel = lax.rem(ids - (me - REACH) * count + whole, whole)
        far = (REACH + DEV // 2) * count
        rel = jnp.where(rel >= far, rel - far + (SLOTS - 1) * count, rel)
        rows_out[start : start + count, 0:189] = jnp.where(ids >= 0, rel + offset, ZERO_ROW)
        kinds_out[start : start + count, 0:189] = kinds[...][:, 0:189] * 4 + level
        start += count
    ids = l3[...]
    rows_out[start : start + 1, 0:189] = jnp.where(ids >= 0, ids + COARSE_ROW, ZERO_ROW)
    kinds_out[start : start + 1, 0:189] = k3[...] * 4 + 3
    for flat, tiled in ((rows_flat, rows_out), (kinds_flat, kinds_out)):
        flat[pl.ds(0, TARGETS, stride=2), :] = tiled[:, 0:128]
        flat[pl.ds(1, TARGETS, stride=2), 0 : SLOT_PAD - 128] = tiled[:, 128:SLOT_PAD]

    live = jnp.where(rows_out[...] != ZERO_ROW, 1.0, 0.0).astype(BF)
    down = jnp.dot(live, jnp.ones((SLOT_PAD, 256), BF), preferred_element_type=F32)[:, :TARGETS]
    across = lax.dot_general(jnp.ones((8, SLOT_PAD), BF), live, NT, preferred_element_type=F32)
    down = (down.astype(I32) + 15) >> 4
    across = (across[0:1].astype(I32) + 15) >> 4
    t_down, t_across = iota((TARGETS, TARGETS), 0), iota((TARGETS, TARGETS), 1)
    before = (across > down) | ((across == down) & (t_across < t_down))
    place = jnp.sum(jnp.where(before, 1.0, 0.0), axis=1, keepdims=True)
    here = place == t_across.astype(F32)
    order = jnp.sum(jnp.where(here, t_down.astype(F32), 0.0), axis=0, keepdims=True).astype(I32)
    meta[...] = jnp.zeros(meta.shape, I32)
    meta[0:1, 0:TARGETS] = order
    sub = iota((16, TARGETS), 0)
    over = jnp.sum(jnp.where(across > sub, 1.0, 0.0), axis=1, keepdims=True).astype(I32)
    ends = jnp.where(iota((16, 256), 1) == iota((16, 256), 0), (over + 3) >> 2, 0)
    meta[1:2, :] = jnp.sum(ends, axis=0, keepdims=True)

    sub_lo = iota((LEAFS, SLOT_PAD), 0)
    sub_hi = iota((32, SLOT_PAD), 0)

    def mark(i, seen):
        lo, hi = [], []
        for k in range(2):
            row = rows_out[pl.ds(2 * i + k, 1), :]
            lo.append(jnp.where(sub_lo == (row & 127), 1.0, 0.0).astype(BF))
            hi.append(jnp.where(sub_hi == (row >> 7), 1.0, 0.0).astype(BF))
        return seen + lax.dot_general(
            jnp.concatenate(hi, axis=0), jnp.concatenate(lo, axis=0), NT, preferred_element_type=F32
        )

    seen = lax.fori_loop(0, LEAFS // 2, mark, jnp.zeros((64, 2 * LEAFS), F32), unroll=4)
    seen = seen[0:32, 0:LEAFS] + seen[32:64, LEAFS:]
    needed = seen > 0.5
    lane = iota((32, LEAFS), 1)
    upto = (
        iota((LEAFS, LEAFS), 0) <= iota((LEAFS, LEAFS), 1)
    )
    rank = jnp.dot(
        jnp.where(needed, 1.0, 0.0).astype(BF),
        jnp.where(upto, 1.0, 0.0).astype(BF),
        preferred_element_type=F32,
    )
    rank = jnp.where(needed, rank, 0.0)
    lane_f = lane.astype(F32)
    asked = jnp.zeros((32, LEAFS), F32)
    for q in range(ROOM):
        pick = jnp.sum(jnp.where(rank == q + 1.0, lane_f, 0.0), axis=1, keepdims=True)
        asked = jnp.where(lane == q, pick, asked)
    asked = asked.astype(I32)
    for h in range(SLOTS):
        req_out[h] = asked[h : h + 1, :]


def plan(lists, kinds):
    return pl.pallas_call(
        plan_kernel,
        out_shape=(
            jax.ShapeDtypeStruct((2 * TARGETS, 128), I32),
            jax.ShapeDtypeStruct((2 * TARGETS, 128), I32),
            jax.ShapeDtypeStruct((SLOTS, 1, 128), I32),
            jax.ShapeDtypeStruct((8, 256), I32),
        ),
        in_specs=[VMEM] * 2 + [ANY] * 6,
        out_specs=[VMEM] * 4,
        scratch_shapes=[pltpu.VMEM((TARGETS, SLOT_PAD), I32)] * 2
        + [pltpu.VMEM((LEAFS, 256), I32)] * 2
        + [pltpu.VMEM((256, LEAFS), I32)]
        + [pltpu.VMEM((n, 189), I32) for n in (16, 2, 1)] * 2
        + [pltpu.SemaphoreType.DMA((6,))],
        compiler_params=pltpu.CompilerParams(vmem_limit_bytes=60 << 20),
        name="plan",
    )(lists[0].T, kinds[0].T, *lists[1:], *kinds[1:])


def left_half():
    return iota((16, 128), 1) < 64


def lift(children, matrices):
    left = left_half()
    zero = jnp.zeros((16, 128), BF)
    rows = [
        jnp.concatenate([jnp.where(left, m, zero), jnp.where(left, zero, m)], axis=0)
        for m in children
    ]
    return lax.dot_general(
        jnp.concatenate(rows, axis=1),
        jnp.concatenate(matrices, axis=1),
        NT,
        preferred_element_type=F32,
    )


def weave(splits):
    lane = iota((32, 128), 1) & 63
    total = None
    for h in range(2):
        put = jnp.where(lane == 2 * iota((32, 128), 0) + h, 1.0, 0.0).astype(BF)
        rows = jnp.concatenate([x[h * 16 : (h + 1) * 16] for x in splits], axis=0)
        part = jnp.dot(rows, put, preferred_element_type=F32)
        total = part if total is None else total + part
    return total.astype(BF)


def unweave(blocks):
    x = jnp.concatenate(blocks, axis=0)
    parts = []
    for h in range(2):
        put = jnp.where(iota((128, 32), 0) == 2 * iota((128, 32), 1) + h, 1.0, 0.0).astype(BF)
        parts.append(jnp.dot(x, put, preferred_element_type=F32))
    return [
        jnp.concatenate([p[i * 16 : (i + 1) * 16] for p in parts], axis=0).astype(BF)
        for i in range(len(blocks))
    ]


def lowered(parent, matrices, locals_):
    left = left_half()
    o = jnp.dot(parent, jnp.concatenate(matrices, axis=1), preferred_element_type=F32)
    fields = []
    for i, local in enumerate(locals_):
        e = o[:, i * 128 : (i + 1) * 128]
        u = jnp.where(left, e[0:16], e[16:32])
        fields.append((local + (u + pltpu.roll(u, 64, 1))).astype(BF))
    return fields


def turn(coupling, weights, first, last, per):
    eye = jnp.where(iota((128, 128), 0) == iota((128, 128), 1), 1.0, 0.0).astype(BF)
    row, col = iota((256, 256), 0), iota((256, 256), 1)
    fits = (col & 63) == 2 * ((row & 127) >> 2) + (row >> 7)
    pick = [
        jnp.where(fits & (((col >> 6) ^ h) == (row & 3)), 1.0, 0.0).astype(BF) for h in range(2)
    ]
    left = iota((32, 128), 1) < 64

    def step(i, c):
        base = (first + i * per) * 4
        rows = [[], []]
        for j in range(2 * per):
            pair = coupling[pl.ds(base + 2 * j, 2)].reshape(256, 128)
            t = lax.dot_general(eye, pair, NT, preferred_element_type=F32).astype(BF)
            for k in range(2):
                y = t[:, k * 128 : (k + 1) * 128]
                for h in range(2):
                    a = y[h * 32 : h * 32 + 32]
                    b = y[64 + h * 32 : 64 + h * 32 + 32]
                    rows[h].append(jnp.concatenate([a, b], axis=1))
        half = [
            jnp.dot(jnp.concatenate(rows[h], axis=0), pick[h], preferred_element_type=F32).astype(BF)
            for h in range(2)
        ]
        for k in range(4 * per):
            for p in range(2):
                a = half[0][k * 32 : k * 32 + 32, p * 128 : (p + 1) * 128]
                b = half[1][k * 32 : k * 32 + 32, p * 128 : (p + 1) * 128]
                weights[base + k, 2 * p] = jnp.where(left, a, b)
                weights[base + k, 2 * p + 1] = jnp.where(left, b, a)
        return c

    lax.fori_loop(0, (last - first) // per, step, 0)


def slot_of(i):
    return i + (i + 15) // 28


def offset_of(p):
    return p - REACH + (DEV // 2 - SLOTS + 1 + REACH) * (p // (SLOTS - 1))


def exchange_kernel(
    req, charges_any, basis_any, transfer_any, coupling_any,
    leaf_out, mu_out, coarse_out, own_leaf, weights_any,
    asked_v, asked_s, send, zbuf, coupling, weights, in_s, out_s,
    charges, basis, leaf, split, mid, part, transfer,
    req_ss, req_rs, loc_s, leaf_ss, leaf_rs, mu_ss, mu_rs, z_ss, z_rs, y_ss, y_rs, x_ss, x_rs,
):
    box = lax.axis_index("boxes")
    grp = lax.axis_index("grp")
    me = box * 4 + grp
    bx = box // 8
    by = box % 8

    def there(p):
        t = (me + offset_of(p) + DEV) % DEV
        return (t // 4, t % 4)

    def back(p):
        t = (me - offset_of(p) + DEV) % DEV
        return (t // 4, t % 4)

    def z_peer(i):
        return (box, (grp + i) % 4)

    def y_peer(i):
        return (bx * 8 + (by + i) % 8, grp)

    def x_peer(i):
        return (((bx + i) % 4) * 8 + by, grp)

    loads = [
        pltpu.make_async_copy(charges_any, charges, in_s.at[0]),
        pltpu.make_async_copy(basis_any, basis, in_s.at[1]),
        pltpu.make_async_copy(coupling_any, coupling, in_s.at[2]),
        pltpu.make_async_copy(transfer_any, transfer, in_s.at[3]),
    ]
    for load in loads:
        load.start()
    barrier = pltpu.get_barrier_semaphore()

    def greet(to, first, count):
        def one(i, c):
            pl.semaphore_signal(barrier, inc=1, device_id=to(i + first), device_id_type=MESH)
            return c

        lax.fori_loop(0, count, one, 0)

    greet(lambda i: there(slot_of(i)), 0, SLOTS - 1)
    greet(z_peer, 1, 3)
    greet(y_peer, 1, 7)
    greet(x_peer, 1, 3)
    pl.semaphore_wait(barrier, SLOTS - 1 + 13)

    def copy(src, dst, ss, rs, to):
        return pltpu.make_async_remote_copy(
            src_ref=src, dst_ref=dst, send_sem=ss, recv_sem=rs, device_id=to, device_id_type=MESH
        )

    def req_copy(p):
        return copy(req.at[p], asked_v.at[p], req_ss.at[p], req_rs.at[p], there(p))

    def leaf_copy(p):
        return copy(send.at[p], leaf_out.at[p], leaf_ss.at[p], leaf_rs.at[p], back(p))

    def mu_copy(p):
        return copy(mu_out.at[REACH], mu_out.at[p], mu_ss.at[p], mu_rs.at[p], back(p))

    def z_copy(i):
        return copy(part, zbuf.at[grp], z_ss.at[i], z_rs.at[i], z_peer(i))

    def y_copy(i):
        own = coarse_out.at[box]
        return copy(own, own, y_ss.at[i], y_rs.at[i], y_peer(i))

    def x_copy(i):
        own = coarse_out.at[pl.ds(bx * 8, 8)]
        return copy(own, own, x_ss.at[i], x_rs.at[i], x_peer(i))

    def each(count, first, act):
        def one(i, c):
            act(i + first)
            return c

        lax.fori_loop(0, count, one, 0)

    each(SLOTS - 1, 0, lambda i: req_copy(slot_of(i)).start())
    left = left_half()
    loads[0].wait()
    loads[1].wait()

    def boxes(i, c):
        for q in range(2):
            b = i * 8 + q * 4
            points = [
                charges[:, pl.ds(pl.multiple_of((b + j) * 256, 256), 256)] for j in range(4)
            ]
            o = lax.dot_general(
                jnp.concatenate(points, axis=0),
                basis[pl.ds(b, 4)].reshape(256, 256),
                NT,
                preferred_element_type=F32,
            )
            for h in range(2):
                lanes = slice(h * 128, (h + 1) * 128)
                pair = jnp.where(
                    left, o[h * 32 : h * 32 + 16, lanes], o[h * 32 + 16 : h * 32 + 32, lanes]
                )
                turned = pltpu.roll(pair, 64, 1)
                leaf[b + 2 * h] = jnp.where(left, pair, turned).astype(BF)
                leaf[b + 2 * h + 1] = jnp.where(left, turned, pair).astype(BF)
                place = pl.ds(pl.multiple_of((i * 4 + q * 2 + h) * 16, 16), 16)
                own_leaf[place, :] = pair.astype(BF)
        return c

    lax.fori_loop(0, LEAFS // 8, boxes, 0)


    def turn_part(k):
        first, last, per = TURN_PARTS[k]
        turn(coupling, weights, first, last, per)
        store_part(k).start()

    def store_part(k):
        span = pl.ds(TURN_PARTS[k][0] * 4, (TURN_PARTS[k][1] - TURN_PARTS[k][0]) * 4)
        return pltpu.make_async_copy(weights.at[span], weights_any.at[span], out_s.at[k])

    loads[3].wait()

    def mids(i, c):
        for k in range(4):
            t = i * 4 + k
            split[t] = lift(
                [leaf[t * 8 + j] for j in range(8)], [transfer[t * 8 + j] for j in range(8)]
            ).astype(BF)
        return c

    lax.fori_loop(0, 4, mids, 0)
    mid[...] = weave([split[t] for t in range(16)]).reshape(16, 16, 128)
    for q in range(8):
        mu_out[REACH, q * 16 : (q + 1) * 16, :] = jnp.where(left, mid[2 * q], mid[2 * q + 1])
    upper = []
    for t in range(2):
        children = range(t * 8, t * 8 + 8)
        sums = lift([mid[j] for j in children], [transfer[128 + j] for j in children])
        upper.append(sums.astype(BF))
    upper = weave(upper)
    upper = [upper[0:16], upper[16:32]]
    mu_out[REACH, 128:144, :] = jnp.where(left, upper[0], upper[1])
    part[...] = jnp.zeros(part.shape, F32)
    part[:, 0:32] = lift(upper, [transfer[144], transfer[145]])
    zbuf[grp] = part[...]
    each(3, 1, lambda i: z_copy(i).start())
    each(SLOTS - 1, 0, lambda i: mu_copy(slot_of(i)).start())
    asked_v[REACH] = jnp.zeros((1, 128), I32)
    each(SLOTS - 1, 0, lambda i: req_copy(slot_of(i)).wait_recv())
    local = pltpu.make_async_copy(asked_v, asked_s, loc_s.at[0])
    local.start()
    local.wait()

    def serve(i):
        p = slot_of(i)
        for q in range(ROOM // 2):
            a = leaf[asked_s[p, 0, 2 * q]]
            b = leaf[asked_s[p, 0, 2 * q + 1]]
            send[p, q * 16 : (q + 1) * 16, :] = jnp.where(left, a, b)
        leaf_copy(p).start()

    each(SLOTS - 1, 0, serve)

    loads[2].wait()
    turn_part(0)
    each(3, 1, lambda i: z_copy(i).wait())
    whole = (zbuf[0] + zbuf[1] + zbuf[2] + zbuf[3]).astype(BF)
    coarse_out[box] = weave([whole[:, 0:32]])
    each(7, 1, lambda i: y_copy(i).start())
    turn_part(1)
    each(7, 1, lambda i: y_copy(i).wait())
    each(3, 1, lambda i: x_copy(i).start())
    turn_part(2)
    each(3, 1, lambda i: x_copy(i).wait())

    each(SLOTS - 1, 0, lambda i: req_copy(slot_of(i)).wait_send())
    each(SLOTS - 1, 0, lambda i: mu_copy(slot_of(i)).wait())
    each(SLOTS - 1, 0, lambda i: leaf_copy(slot_of(i)).wait())
    for k in range(len(TURN_PARTS)):
        store_part(k).wait()


def exchange(req, charges, basis, transfer, coupling):
    sem = pltpu.SemaphoreType.DMA
    return pl.pallas_call(
        exchange_kernel,
        out_shape=(
            jax.ShapeDtypeStruct((SLOTS, 256, 128), BF),
            jax.ShapeDtypeStruct((SLOTS, 144, 128), BF),
            jax.ShapeDtypeStruct((32, 16, 128), BF),
            jax.ShapeDtypeStruct((1024, 128), BF),
            jax.ShapeDtypeStruct((KINDS, 4, 32, 128), BF),
        ),
        in_specs=[VMEM] + [ANY] * 4,
        out_specs=[VMEM] * 4 + [ANY],
        scratch_shapes=[
            pltpu.VMEM((SLOTS, 1, 128), I32),
            pltpu.SMEM((SLOTS, 1, 128), I32),
            pltpu.VMEM((SLOTS, 256, 128), BF),
            pltpu.VMEM((4, 32, 128), F32),
            pltpu.VMEM((KINDS, 128, 128), BF),
            pltpu.VMEM((KINDS, 4, 32, 128), BF),
            sem((4,)),
            sem((len(TURN_PARTS),)),
            pltpu.VMEM((16, 32768), BF),
            pltpu.VMEM((LEAFS, 64, 256), BF),
            pltpu.VMEM((LEAFS, 16, 128), BF),
            pltpu.VMEM((16, 32, 32), BF),
            pltpu.VMEM((16, 16, 128), BF),
            pltpu.VMEM((32, 128), F32),
            pltpu.VMEM((146, 32, 128), BF),
        ]
        + [sem((SLOTS,))] * 7
        + [sem((8,))] * 6,
        compiler_params=pltpu.CompilerParams(
            collective_id=0, has_side_effects=True, vmem_limit_bytes=60 << 20
        ),
        name="exchange",
    )(req, charges, basis, transfer, coupling)


def far_kernel(
    req, meta, own_leaf, leaf_in, mu_in, coarse_in,
    rows_any, kinds_any, weights_any, basis_any, transfer_any, out,
    rows_idx, kinds_idx, table, weights, basis, transfer, local, parents, in_s,
):
    loads = [
        pltpu.make_async_copy(rows_any, rows_idx, in_s.at[0]),
        pltpu.make_async_copy(kinds_any, kinds_idx, in_s.at[1]),
        pltpu.make_async_copy(weights_any, weights, in_s.at[2]),
    ]
    load_basis = pltpu.make_async_copy(basis_any, basis, in_s.at[3])
    load_transfer = pltpu.make_async_copy(transfer_any, transfer, in_s.at[4])
    for load in loads:
        load.start()
    l = iota((128, 512), 0)
    n = iota((128, 512), 1)
    spread = jnp.where(l == (n >> 7) * 32 + (n & 31), 1.0, 0.0).astype(BF)
    table[ZERO_ROW] = jnp.zeros((32, 128), BF)

    def fill(block, places):
        y = jnp.dot(block, spread, preferred_element_type=F32).astype(BF)
        for i, (a, b, h) in enumerate(places):
            s = slice(i * 16, (i + 1) * 16)
            first = [y[s, 0:128], y[s, 128:256]]
            table[a] = jnp.concatenate([first[h], first[1 - h]], axis=0)
            if b is not None:
                last = [y[s, 256:384], y[s, 384:512]]
                table[b] = jnp.concatenate([last[h], last[1 - h]], axis=0)

    def mu_places(p):
        mid = [(MID_ROW + p * 16 + 2 * i, MID_ROW + p * 16 + 2 * i + 1, 1) for i in range(8)]
        return mid + [(UPPER_ROW + p * 2, UPPER_ROW + p * 2 + 1, 0)]

    def peers(i, c):
        for k in range(3):
            peer(i * 3 + k)
        return c

    def peer(i):
        p = slot_of(i)
        fill(
            leaf_in[p],
            [
                (p * LEAFS + req[p, 0, 2 * q], p * LEAFS + req[p, 0, 2 * q + 1], 0)
                for q in range(16)
            ],
        )
        fill(mu_in[p], mu_places(p))

    lax.fori_loop(0, (SLOTS - 1) // 3, peers, 0)
    fill(mu_in[REACH], mu_places(REACH))

    def own(i, c):
        base = REACH * LEAFS + i * 32
        fill(
            own_leaf[pl.ds(pl.multiple_of(i * 256, 256), 256), :],
            [(base + 2 * q, base + 2 * q + 1, 0) for q in range(16)],
        )
        return c

    lax.fori_loop(0, 4, own, 0)

    def coarse(i, c):
        fill(
            coarse_in[pl.ds(pl.multiple_of(i * 128, 128), 128), :],
            [(COARSE_ROW + i * 8 + q, None, 1) for q in range(8)],
        )
        return c

    lax.fori_loop(0, 4, coarse, 0)

    for load in loads:
        load.wait()
    load_basis.start()
    load_transfer.start()
    lane = iota((32, 128), 1)
    m1, m2, m3 = lane < 32, lane < 64, lane < 96
    left = iota((16, 128), 1) < 64

    def merge(a, b, c, d):
        return jnp.where(m2, jnp.where(m1, a, b), jnp.where(m3, c, d))

    def one(t, batches):
        acc = None
        for b in range(batches):
            cols, quads = [], []
            for g in range(2):
                base = b * 16 + g * 8
                cols.append(
                    jnp.concatenate([weights[kinds_idx[t * 256 + base + j]] for j in range(8)], axis=0)
                )
                quads.append(
                    jnp.concatenate(
                        [
                            merge(*[table[rows_idx[t * 256 + base + q * 4 + i]] for i in range(4)])
                            for q in range(2)
                        ],
                        axis=1,
                    )
                )
            d = jnp.dot(
                jnp.concatenate(quads, axis=0),
                jnp.concatenate(cols, axis=1),
                preferred_element_type=F32,
            )
            acc = d if acc is None else acc + d
        u = jnp.where(
            left, acc[0:16, 0:128] + acc[32:48, 128:256], acc[16:32, 0:128] + acc[48:64, 128:256]
        )
        local[t] = u + pltpu.roll(u, 64, 1)

    def four(i, c, batches):
        for k in range(4):
            one(meta[0, i * 4 + k], batches)
        return c

    first = 0
    for batches in range(SLOT_PAD // 16, 5, -1):
        last = meta[1, batches - 1] if batches > 6 else TARGETS // 4
        lax.fori_loop(first, last, functools.partial(four, batches=batches), 0)
        first = last

    load_basis.wait()
    load_transfer.wait()
    (coarse_field,) = unweave([local[146].astype(BF)])
    upper_fields = unweave(
        lowered(coarse_field, [transfer[144], transfer[145]], [local[144], local[145]])
    )
    mid_fields = []
    for u in range(2):
        children = range(u * 8, u * 8 + 8)
        mid_fields += lowered(
            upper_fields[u], [transfer[128 + m] for m in children], [local[128 + m] for m in children]
        )
    for m, field in enumerate(unweave(mid_fields)):
        parents[m] = field

    zero = jnp.zeros((16, 128), BF)

    def boxes(m):
        fields = lowered(
            parents[m],
            [transfer[m * 8 + j] for j in range(8)],
            [local[m * 8 + j] for j in range(8)],
        )
        for q in range(2):
            rows = []
            for j in range(4):
                f = fields[q * 4 + j]
                f = jnp.where(left, zero, f) if j % 2 else jnp.where(left, f, zero)
                rows.append(jnp.concatenate([zero, f] if j > 1 else [f, zero], axis=1))
            b = m * 8 + q * 4
            points = jnp.dot(
                jnp.concatenate(rows, axis=0),
                basis[pl.ds(b, 4)].reshape(256, 256),
                preferred_element_type=F32,
            ).astype(BF)
            for j in range(4):
                place = pl.ds(pl.multiple_of((b + j) * 256, 256), 256)
                out[:, place] = points[j * 16 : (j + 1) * 16]

    def two(i, c):
        boxes(2 * i)
        boxes(2 * i + 1)
        return c

    lax.fori_loop(0, 8, two, 0)


def far(rows_idx, kinds_idx, req, meta, own_leaf, leaf_in, mu_in, coarse_in, transfer, weights, basis):
    return pl.pallas_call(
        far_kernel,
        out_shape=jax.ShapeDtypeStruct((16, LEAFS * 256), BF),
        in_specs=[SMEM] * 2 + [VMEM] * 4 + [ANY] * 5,
        out_specs=VMEM,
        scratch_shapes=[
            pltpu.SMEM((TARGETS * 256,), I32),
            pltpu.SMEM((TARGETS * 256,), I32),
            pltpu.VMEM((TABLE_ROWS, 32, 128), BF),
            pltpu.VMEM((4 * KINDS, 32, 128), BF),
            pltpu.VMEM((LEAFS, 64, 256), BF),
            pltpu.VMEM((146, 32, 128), BF),
            pltpu.VMEM((TARGETS, 16, 128), F32),
            pltpu.VMEM((16, 32, 32), BF),
            pltpu.SemaphoreType.DMA((5,)),
        ],
        compiler_params=pltpu.CompilerParams(vmem_limit_bytes=60 << 20),
        name="far",
    )(
        req, meta, own_leaf, leaf_in, mu_in, coarse_in, rows_idx, kinds_idx, weights, basis, transfer
    )


def on_device(
    charges, leaf_basis, transfer0, transfer1, transfer2, coupling,
    lists0, lists1, lists2, lists3, kinds0, kinds1, kinds2, kinds3,
):
    transfer = jnp.concatenate([transfer0, transfer1, transfer2], axis=0).reshape(146, 32, 128)
    by_kind = coupling.reshape(4, KINDS, 32, 128).transpose(1, 2, 0, 3).reshape(KINDS, 128, 128)
    rows_idx, kinds_idx, req, meta = plan(
        (lists0, lists1, lists2, lists3), (kinds0, kinds1, kinds2, kinds3)
    )
    leaf_in, mu_in, coarse_in, own_leaf, weights = exchange(
        req, charges, leaf_basis, transfer, by_kind
    )
    return far(
        rows_idx.reshape(-1), kinds_idx.reshape(-1), req, meta, own_leaf, leaf_in, mu_in,
        coarse_in.reshape(512, 128), transfer, weights.reshape(4 * KINDS, 32, 128), leaf_basis,
    )


def solution(mesh):
    both = ("boxes", "grp")
    in_specs = (
        P(None, both),
        P(both, None, None),
        P(both, None),
        P(both, None),
        P(both, None),
        P(),
        P(both, None),
        P(both, None),
        P(both, None),
        P("boxes", None),
        P(both, None),
        P(both, None),
        P(both, None),
        P("boxes", None),
    )
    return jax.shard_map(
        on_device, mesh=mesh, in_specs=in_specs, out_specs=P(None, both), check_vma=False
    )
```
